256 devices in a mesh: row: 64 (over z, y, x_hi), col: 2 (over core), layer: 2 (over x_lo).
Axes of the slice: x: 4 (x_hi: 2, x_lo: 2; x = x_hi * 2 + x_lo), y: 4, z: 8, core: 2. Of those that a mesh axis runs over, the one named last changes fastest.
Arguments:
- matrix: float32 [1, 64, 256, 32, 2, 256], P(None, 'row', None, None, 'col'), may hold values from -8 to 113.137085, as said below
Outputs:
- factored: float32 [1, 64, 256, 32, 2, 256], P(None, 'row', None, 'layer', 'col')
The draws below stay inside these ranges and needn't reach their ends.
Inputs may be any that keep to these rules, and one draw needn't show every extreme that they name: `matrix`: viewed as in the first step it is symmetric, its leading 2 * 256 x 2 * 256 block is positive definite, and its diagonal entries lie between 2.5 and 5 times the square root of 512.
All inputs are finite; a program needn't handle non-finite values.
Results may differ from the reference program's by a relative error of at most 0.000059.
Values sent between devices are 32-bit elements; how exact they have to be, the bound alone decides.
A program may use at most 128 MiB of HBM per device.

```python
import math
import jax
import jax.numpy as jnp
from jax import lax

BS = 256
RB = 1
ORDER = 16384
CB = 32
N_ROW = 64
N_COL = 2


def draw_matrix(key, part):
    first_key, second_key = jax.random.split(jax.random.fold_in(key, 17))
    base = jnp.clip(jax.random.normal(first_key, (ORDER, ORDER), jnp.float32), -5.0, 5.0)
    scales = jnp.exp(jax.random.uniform(second_key, (ORDER,), jnp.float32, math.log(2.5), math.log(5.0)))
    symmetric = (base + base.T) * 0.70710678
    rows = lax.broadcasted_iota(jnp.int32, (ORDER, ORDER), 0)
    cols = lax.broadcasted_iota(jnp.int32, (ORDER, ORDER), 1)
    whole = jnp.where(rows == cols, (scales * math.sqrt(2.0 * BS))[None, :], symmetric)
    return whole.reshape(RB, N_ROW, BS, CB, N_COL, BS)


def setup_inputs(seed: int = 0) -> dict:
    arg_keys = jax.random.split(jax.random.key(seed), 2)
    matrix = draw_matrix(jax.random.fold_in(arg_keys[1], 71), 0)
    return dict(matrix=matrix)


HIGH = lax.Precision.HIGHEST

def factor_block(diag_block):
    lower_fac = jnp.linalg.cholesky(diag_block)
    identity = jnp.eye(diag_block.shape[0], dtype=jnp.float32)
    inverse = lax.linalg.triangular_solve(lower_fac, identity, left_side=True, lower=True)
    return (lower_fac, inverse)

def product(left, right):
    return jnp.dot(left.astype(jnp.float32), right.astype(jnp.float32), precision=HIGH, preferred_element_type=jnp.float32)

def reference(matrix):
    work = matrix.reshape(ORDER, ORDER)
    lower_first, inverse_first = factor_block(work[:BS, :BS])
    panel_first = jnp.concatenate([lower_first, product(work[BS:, :BS], inverse_first.T)], axis=0)
    column_next = work[:, BS:2 * BS] - product(panel_first, panel_first[BS:2 * BS].T)
    lower_next, inverse_next = factor_block(column_next[BS:2 * BS])
    panel_next = jnp.concatenate([jnp.zeros((BS, BS), jnp.float32), lower_next, product(column_next[2 * BS:], inverse_next.T)], axis=0)
    panels = jnp.concatenate([panel_first, panel_next], axis=1)
    rest = work[:, 2 * BS:] - product(panels, panels[2 * BS:].T)
    return jnp.concatenate([panels, rest], axis=1).reshape(matrix.shape)
```

```python
import jax
import jax.numpy as jnp
from jax import lax
from jax.experimental import pallas as pl
from jax.experimental.pallas import tpu as pltpu
from jax.sharding import PartitionSpec as P

HIGH = lax.Precision.HIGHEST
BS = 256
LEAD = 2 * BS
NB = 128
ZROWS = 88
YROWS = 40
YBASE = 2 * ZROWS
MESH = pl.DeviceIdType.MESH


def dotf(a, b, ca, cb):
    return lax.dot_general(
        a, b, (((ca,), (cb,)), ((), ())), precision=HIGH, preferred_element_type=jnp.float32
    )


def diag_factor(dx, between):
    sub = lax.broadcasted_iota(jnp.int32, (8, NB), 0)
    for p in range(NB // 8):
        lo = 8 * p
        left = dx[lo : lo + 8, 0:NB]
        right = dx[lo : lo + 8, NB : 2 * NB]
        cols = [jnp.broadcast_to(left[:, lo + i : lo + i + 1], (8, NB)) for i in range(8)]
        for i in range(8):
            pivot = jnp.broadcast_to(cols[i][i : i + 1, :], (8, NB))
            root = lax.rsqrt(pivot)
            keep = jnp.where(sub == i, root, 1.0)
            mult = jnp.where(sub > i, cols[i] * (root * root), 0.0)
            for k in range(i + 1, 8):
                row = jnp.broadcast_to(cols[k][i : i + 1, :], (8, NB))
                cols[k] = cols[k] * keep - mult * row
            left = left * keep - mult * jnp.broadcast_to(left[i : i + 1, :], (8, NB))
            right = right * keep - mult * jnp.broadcast_to(right[i : i + 1, :], (8, NB))
        both = jnp.concatenate([left, right], axis=1)
        dx[lo : lo + 8, :] = both
        if p < NB // 8 - 1:
            upd = dotf(left, both, 0, 0)
            dx[lo + 8 :, :] = dx[lo + 8 :, :] - upd[lo + 8 :, :]
        between(p)


def gather_kernel(
    col0, g, q_out, p_out, w, abuf, m, dx,
    inj_send, inj_recv, w_send, w_recv,
    sc_send, sc_recv, ag_send, ag_recv, sib_send, sib_recv,
    z_send, z_recv, yz_send, yz_recv, yy_send, yy_recv, loc,
):
    row = lax.axis_index("row")
    core = lax.axis_index("col")
    xlo = lax.axis_index("layer")
    z = row // 8
    y = (row // 2) % 4
    xhi = row % 2
    x = xhi * 2 + xlo
    n = z * 4 + y

    def dev(dz, dy, dx_, dc):
        return {"row": dz * 8 + dy * 2 + dx_ // 2, "col": dc, "layer": dx_ % 2}

    def remote(src, dst, ss, rs, to):
        return pltpu.make_async_remote_copy(
            src_ref=src, dst_ref=dst, send_sem=ss, recv_sem=rs, device_id=to, device_id_type=MESH
        )

    sibling = dev(z, y, x, 1 - core)

    unit = xhi + core
    is_src = (row < 2) & ((xhi == 0) | (core == 1))
    own_src = (row == 0) & (core == 0)
    match = n % 2 == core

    @pl.when(is_src)
    def _():
        def one(i, _):
            src = col0.at[pl.ds(pl.multiple_of(8 * i, 8), 8), :]
            dst = abuf.at[unit, i // 2, i % 2]

            @pl.when((i == 0) & own_src)
            def _():
                pltpu.make_async_copy(src, dst, sc_recv.at[unit]).start()

            @pl.when(jnp.logical_not((i == 0) & own_src))
            def _():
                remote(src, dst, sc_send.at[0], sc_recv.at[unit], dev(i // 4, i % 4, x, i % 2)).start()

            remote(src, dst, sc_send.at[0], sc_recv.at[unit], dev(i // 4, i % 4, 3 - x, i % 2)).start()
            return 0

        lax.fori_loop(0, 32, one, 0)

    zhalf = z // 4
    same = xlo == zhalf
    inj_x = jnp.where(same, x, 3 - x)
    inj_self = same & (xhi == core)
    own_slot = (z % 4) * 4 + y
    inj_dst = g.at[pl.ds(pl.multiple_of(own_slot * BS, BS), BS), pl.ds(pl.multiple_of(core * BS, BS), BS)]
    inj = remote(col0, inj_dst, inj_send.at[0], inj_recv.at[core], dev(z, y, inj_x, xhi))
    inj_local = pltpu.make_async_copy(col0, inj_dst, inj_recv.at[core])

    @pl.when(inj_self)
    def _():
        inj_local.start()

    @pl.when(jnp.logical_not(inj_self))
    def _():
        inj.start()

    w_copy = remote(col0, w.at[core], w_send.at[0], w_recv.at[0], sibling)
    w_copy.start()
    w_local = pltpu.make_async_copy(col0, w.at[core], loc.at[0])
    w_local.start()

    def spread(which, first, count):
        @pl.when(match)
        def _():
            for u in range(first, first + count):
                pltpu.make_async_copy(
                    abuf.at[u, n // 2, core], abuf.at[u, n // 2, core], sc_recv.at[u]
                ).wait()
            piece = abuf.at[pl.ds(first, count), n // 2, core]

            def one(i, _):
                other = (n + i) % 32
                remote(piece, piece, ag_send.at[which], ag_recv.at[which], dev(other // 4, other % 4, x, core)).start()
                return 0

            lax.fori_loop(1, 32, one, 0)

    spread(0, 0, 1)
    spread(1, 1, 2)

    def bytes_wait(sem, pieces):
        ref = m.at[0 : 8 * pieces, 0:BS]
        pltpu.make_async_copy(ref, ref, sem).wait()

    def sib_copy(which, first, count):
        half = abuf.at[pl.ds(first, count), :, core]
        return remote(half, half, sib_send.at[which], sib_recv.at[which], sibling)

    def lead_half(which, first, count):
        @pl.when(match)
        def _():
            bytes_wait(ag_recv.at[which], 15 * count)

        @pl.when(jnp.logical_not(match))
        def _():
            bytes_wait(ag_recv.at[which], 16 * count)

        sib_copy(which, first, count).start()

    zp = (z + 8 - 4 * xlo) % 8
    near = zp < 4
    far = jnp.logical_not(near)
    zd = (zp, (11 - zp) % 8)
    base = tuple(jnp.where(v < 4, v, 3) for v in zd)
    nsend = tuple(jnp.where((v <= 2) | (v == 7), 3, 4) for v in zd)
    zto = (dev((z + 1) % 8, y, x, core), dev((z + 7) % 8, y, x, core))
    yup = dev(z, (y + 1) % 4, x, core)
    ydown = dev(z, (y + 3) % 4, x, core)
    yto = (yup, ydown)
    yfrom = ((y + 3) % 4, (y + 1) % 4)
    gray = (0, 1, 3, 2)
    yslot = {1: 1, 3: 0, 2: 2}

    def source_z(d, q):
        s = (base[d] + 4 - q) % 4
        return s if d == 0 else 3 - s

    def part(zs, ys, first, rows):
        start = (zs * 4 + ys) * BS + first
        return g.at[pl.ds(pl.multiple_of(start, 8), rows), :]

    def zpart(d, q, ys):
        return part(source_z(d, q), ys, ZROWS * d, ZROWS)

    def ypart(d, zs, ys):
        return part(zs, ys, YBASE + YROWS * d, YROWS)

    def zchunk(d, q, j):
        if j == 0:
            return zpart(d, q, y)
        return ypart(d, source_z(d, q), (y + gray[j - 1]) % 4)

    def zcopy(d, q, j, ref):
        return remote(ref, ref, z_send.at[d, q, j], z_recv.at[d, q, j], zto[d])

    def yz_copy(d, q, s, ref, to):
        return remote(ref, ref, yz_send.at[d, q, s], yz_recv.at[d, q, s], to)

    def yy_copy(d, s, ref, to):
        return remote(ref, ref, yy_send.at[d, s], yy_recv.at[d, s], to)

    def near_start():
        @pl.when(near)
        def _():
            for h in range(2):
                pltpu.make_async_copy(col0, col0, inj_recv.at[h]).wait()
            for d in range(2):
                ref = ypart(d, z % 4, y)
                yy_copy(d, 0, ref, yup).start()
                yy_copy(d, 1, ref, ydown).start()

    def near_forward():
        @pl.when(near)
        def _():
            for d in range(2):
                ref = ypart(d, z % 4, yfrom[d])
                yy_copy(d, d, ref, yto[d]).wait_recv()
                yy_copy(d, 2, ref, yto[d]).start()

    def event(d, q, j):
        ref = zchunk(d, q, j)

        @pl.when(near & (q > 0))
        def _():
            pltpu.make_async_copy(ref, ref, z_recv.at[d, jnp.maximum(q - 1, 0), j]).wait()

        @pl.when(far)
        def _():
            pltpu.make_async_copy(ref, ref, z_recv.at[d, q, j]).wait()

        if j > 1 and yslot[gray[j - 1]] != d:
            @pl.when(near & (q == 0))
            def _():
                pltpu.make_async_copy(ref, ref, yy_recv.at[d, yslot[gray[j - 1]]]).wait()

        @pl.when(q < nsend[d])
        def _():
            zcopy(d, q, j, ref).start()

        if j == 0:
            yz_copy(d, q, 0, ref, yup).start()
            yz_copy(d, q, 1, ref, ydown).start()

    def y_forward(d, q):
        ref = zpart(d, q, yfrom[d])
        yz_copy(d, q, d, ref, yto[d]).wait_recv()
        yz_copy(d, q, 2, ref, yto[d]).start()

    def finish():
        inj_wait = jnp.logical_not(inj_self)

        @pl.when(inj_wait)
        def _():
            inj.wait_send()

        w_copy.wait_send()

        @pl.when(is_src)
        def _():
            @pl.when(own_src)
            def _():
                bytes_wait(sc_send.at[0], 63)

            @pl.when(jnp.logical_not(own_src))
            def _():
                bytes_wait(sc_send.at[0], 64)

        @pl.when(match)
        def _():
            bytes_wait(ag_send.at[0], 31)
            bytes_wait(ag_send.at[1], 62)

        for which, first, count in ((0, 0, 1), (1, 1, 2)):
            sib_copy(which, first, count).wait_send()

        @pl.when(near)
        def _():
            for d in range(2):
                for s in range(3):
                    yy_copy(d, s, ypart(d, z % 4, y), yup).wait_send()

        def each(q, _):
            for d in range(2):
                for s in range(3):
                    copy = yz_copy(d, q, s, zpart(d, q, y), yup)
                    copy.wait_send()
                    if s != d:
                        copy.wait_recv()

                @pl.when(q < nsend[d])
                def _():
                    for j in range(5):
                        zcopy(d, q, j, zchunk(d, q, j)).wait_send()
            return 0

        lax.fori_loop(0, 4, each, 0)

    near_start()

    def comm(q, _):
        for j in range(5):
            for d in range(2):
                event(d, q, j)
            if j == 1:
                @pl.when(q == 0)
                def _():
                    near_forward()
        for d in range(2):
            y_forward(d, q)
        return 0

    lax.fori_loop(0, 4, comm, 0)

    eye = (
        lax.broadcasted_iota(jnp.int32, (LEAD, LEAD), 0)
        == lax.broadcasted_iota(jnp.int32, (LEAD, LEAD), 1)
    ).astype(jnp.float32)
    m[:, LEAD:] = eye
    lead_half(0, 0, 1)
    lead_half(1, 1, 2)
    for which, first, count in ((0, 0, 1), (1, 1, 2)):
        sib_copy(which, first, count).wait_recv()
    m[0:BS, 0:BS] = abuf[0].reshape(BS, BS)
    m[0:BS, BS:LEAD] = abuf[1].reshape(BS, BS)
    m[BS:LEAD, BS:LEAD] = abuf[2].reshape(BS, BS)
    m[BS:LEAD, 0:BS] = jnp.zeros((BS, BS), jnp.float32)

    def step(k, _):
        off = pl.multiple_of(k * NB, NB)
        dx[:, 0:NB] = m[pl.ds(off, NB), pl.ds(off, NB)]
        dx[:, NB : 2 * NB] = eye[0:NB, 0:NB]
        diag_factor(dx, lambda p: None)
        mk = dotf(dx[:, NB : 2 * NB], m[pl.ds(off, NB), :], 1, 0)
        m[pl.ds(off, NB), :] = mk

        def trail(i, _):
            oi = pl.multiple_of(i * NB, NB)
            u = m[pl.ds(off, NB), pl.ds(oi, NB)]
            m[pl.ds(oi, NB), :] = m[pl.ds(oi, NB), :] - dotf(u, mk, 0, 0)
            return 0

        lax.fori_loop(k + 1, LEAD // NB, trail, 0)
        return 0

    lax.fori_loop(0, LEAD // NB, step, 0)

    w_copy.wait_recv()
    w_local.wait()
    p0 = dotf(w[0], m[0:BS, LEAD : LEAD + BS], 1, 1)
    p1 = dotf(w[0], m[BS:LEAD, LEAD : LEAD + BS], 1, 1) + dotf(w[1], m[BS:LEAD, LEAD + BS :], 1, 1)
    q_out[:, 0:BS] = dotf(p0, m[0:BS, LEAD : LEAD + BS], 1, 0) + dotf(p1, m[BS:LEAD, LEAD : LEAD + BS], 1, 0)
    q_out[:, BS:LEAD] = dotf(p1, m[BS:LEAD, LEAD + BS :], 1, 0)
    p_out[...] = jnp.where(core == 0, p0, p1)
    ri = lax.broadcasted_iota(jnp.int32, (BS, BS), 0)
    ci = lax.broadcasted_iota(jnp.int32, (BS, BS), 1)

    @pl.when((row == 0) & (core == 0))
    def _():
        p_out[...] = jnp.where(ri >= ci, m[0:BS, 0:BS].T, 0.0)

    @pl.when((row == 0) & (core == 1))
    def _():
        p_out[...] = jnp.zeros((BS, BS), jnp.float32)

    @pl.when((row == 1) & (core == 0))
    def _():
        p_out[...] = m[0:BS, BS:LEAD].T

    @pl.when((row == 1) & (core == 1))
    def _():
        p_out[...] = jnp.where(ri >= ci, m[BS:LEAD, BS:LEAD].T, 0.0)

    finish()


def gather_and_factor(col0):
    dma = pltpu.SemaphoreType.DMA
    vmem = pl.BlockSpec(memory_space=pltpu.VMEM)
    return pl.pallas_call(
        gather_kernel,
        out_shape=(
            jax.ShapeDtypeStruct((16 * BS, LEAD), jnp.float32),
            jax.ShapeDtypeStruct((BS, LEAD), jnp.float32),
            jax.ShapeDtypeStruct((BS, BS), jnp.float32),
        ),
        in_specs=[vmem],
        out_specs=(pl.BlockSpec(memory_space=pl.ANY), vmem, vmem),
        scratch_shapes=[
            pltpu.VMEM((2, BS, BS), jnp.float32),
            pltpu.VMEM((3, 16, 2, 8, BS), jnp.float32),
            pltpu.VMEM((LEAD, 2 * LEAD), jnp.float32),
            pltpu.VMEM((NB, 2 * NB), jnp.float32),
            dma((1,)), dma((2,)), dma((1,)), dma((1,)),
            dma((1,)), dma((3,)), dma((2,)), dma((2,)), dma((2,)), dma((2,)),
            dma((2, 4, 5)), dma((2, 4, 5)), dma((2, 4, 3)), dma((2, 4, 3)), dma((2, 3)), dma((2, 3)),
            dma((1,)),
        ],
        compiler_params=pltpu.CompilerParams(has_side_effects=True, vmem_limit_bytes=40 << 20),
        cost_estimate=pl.CostEstimate(flops=2 * LEAD**3, bytes_accessed=16 << 20, transcendentals=LEAD),
    )(col0)


def update_kernel(layer, base, g, q, panel, out):
    step = pl.program_id(0)
    for b in range(4):
        upd = dotf(q[...], g[b * BS : (b + 1) * BS, :], 1, 1)
        for h in range(2):
            s = 2 * b + h
            out[:, s, :] = base[:, s, :] - upd[:, h * 128 : (h + 1) * 128]

    @pl.when((step == 0) & (layer[0] == 0))
    def _():
        for h in range(2):
            out[:, h, :] = panel[:, h * 128 : (h + 1) * 128]


def update(layer, tile, g, q, panel):
    return pl.pallas_call(
        update_kernel,
        out_shape=jax.ShapeDtypeStruct((BS, 32, 128), jnp.float32),
        grid_spec=pltpu.PrefetchScalarGridSpec(
            num_scalar_prefetch=1,
            grid=(4,),
            in_specs=[
                pl.BlockSpec((BS, 8, 128), lambda i, lay: (0, lay[0] * 4 + i, 0)),
                pl.BlockSpec((4 * BS, LEAD), lambda i, lay: (i, 0)),
                pl.BlockSpec((BS, LEAD), lambda i, lay: (0, 0)),
                pl.BlockSpec((BS, BS), lambda i, lay: (0, 0)),
            ],
            out_specs=pl.BlockSpec((BS, 8, 128), lambda i, lay: (0, i, 0)),
        ),
        compiler_params=pltpu.CompilerParams(vmem_limit_bytes=40 << 20),
        cost_estimate=pl.CostEstimate(flops=2 * BS * LEAD * 16 * BS, bytes_accessed=16 << 20, transcendentals=0),
    )(layer, tile, g, q, panel)


def on_device(matrix):
    tile = matrix.reshape(BS, 64, 128)
    col0 = tile[:, 0:2, :].reshape(BS, BS)
    g, q, panel = gather_and_factor(col0)
    layer = lax.axis_index("layer").reshape(1).astype(jnp.int32)
    out = update(layer, tile, g, q, panel)
    return out.reshape(1, 1, BS, 16, 1, BS)


def solution(mesh):
    in_specs = (P(None, "row", None, None, "col", None),)
    out_specs = P(None, "row", None, "layer", "col", None)
    return jax.shard_map(
        on_device, mesh=mesh, in_specs=in_specs, out_specs=out_specs, check_vma=False
    )
```

```python
import jax
import jax.numpy as jnp
from jax import lax
from jax.experimental import pallas as pl
from jax.experimental.pallas import tpu as pltpu
from jax.sharding import PartitionSpec as P

HIGH = lax.Precision.HIGHEST
BS = 256
LEAD = 2 * BS
NB = 128
ZROWS = 40
YROWS = 48
YBASE = 4 * ZROWS
EVENTS = 24
SLOTS = 32
MESH = pl.DeviceIdType.MESH


def dotf(a, b, ca, cb):
    return lax.dot_general(
        a, b, (((ca,), (cb,)), ((), ())), precision=HIGH, preferred_element_type=jnp.float32
    )


def diag_factor(dx, between):
    sub = lax.broadcasted_iota(jnp.int32, (8, NB), 0)
    for p in range(NB // 8):
        lo = 8 * p
        left = dx[lo : lo + 8, 0:NB]
        right = dx[lo : lo + 8, NB : 2 * NB]
        cols = [jnp.broadcast_to(left[:, lo + i : lo + i + 1], (8, NB)) for i in range(8)]
        for i in range(8):
            pivot = jnp.broadcast_to(cols[i][i : i + 1, :], (8, NB))
            root = lax.rsqrt(pivot)
            keep = jnp.where(sub == i, root, 1.0)
            mult = jnp.where(sub > i, cols[i] * (root * root), 0.0)
            for k in range(i + 1, 8):
                row = jnp.broadcast_to(cols[k][i : i + 1, :], (8, NB))
                cols[k] = cols[k] * keep - mult * row
            left = left * keep - mult * jnp.broadcast_to(left[i : i + 1, :], (8, NB))
            right = right * keep - mult * jnp.broadcast_to(right[i : i + 1, :], (8, NB))
        both = jnp.concatenate([left, right], axis=1)
        dx[lo : lo + 8, :] = both
        if p < NB // 8 - 1:
            upd = dotf(left, both, 0, 0)
            dx[lo + 8 :, :] = dx[lo + 8 :, :] - upd[lo + 8 :, :]
        between(p)


def gather_kernel(
    col0, g, q_out, p_out, w, abuf, m, dx,
    inj_send, inj_recv, w_send, w_recv,
    sc_send, sc_recv, ag_send, ag_recv, sib_send, sib_recv,
    z_send, z_recv, yz_send, yz_recv, yy_send, yy_recv, loc,
):
    row = lax.axis_index("row")
    core = lax.axis_index("col")
    xlo = lax.axis_index("layer")
    z = row // 8
    y = (row // 2) % 4
    xhi = row % 2
    x = xhi * 2 + xlo
    n = z * 4 + y

    def dev(dz, dy, dx_, dc):
        return {"row": dz * 8 + dy * 2 + dx_ // 2, "col": dc, "layer": dx_ % 2}

    def remote(src, dst, ss, rs, to):
        return pltpu.make_async_remote_copy(
            src_ref=src, dst_ref=dst, send_sem=ss, recv_sem=rs, device_id=to, device_id_type=MESH
        )

    sibling = dev(z, y, x, 1 - core)

    unit = xhi + core
    is_src = (row < 2) & ((xhi == 0) | (core == 1))
    own_src = (row == 0) & (core == 0)
    match = n % 2 == core

    @pl.when(is_src)
    def _():
        def one(i, _):
            src = col0.at[pl.ds(pl.multiple_of(8 * i, 8), 8), :]
            dst = abuf.at[unit, i // 2, i % 2]

            @pl.when((i == 0) & own_src)
            def _():
                pltpu.make_async_copy(src, dst, sc_recv.at[unit]).start()

            @pl.when(jnp.logical_not((i == 0) & own_src))
            def _():
                remote(src, dst, sc_send.at[0], sc_recv.at[unit], dev(i // 4, i % 4, x, i % 2)).start()

            remote(src, dst, sc_send.at[0], sc_recv.at[unit], dev(i // 4, i % 4, 3 - x, i % 2)).start()
            return 0

        lax.fori_loop(0, 32, one, 0)

    zhalf = z // 4
    same = xlo == zhalf
    inj_x = jnp.where(same, x, 3 - x)
    inj_self = same & (xhi == core)
    own_slot = (z % 4) * 4 + y
    inj_dst = g.at[pl.ds(pl.multiple_of(own_slot * BS, BS), BS), pl.ds(pl.multiple_of(core * BS, BS), BS)]
    inj = remote(col0, inj_dst, inj_send.at[0], inj_recv.at[core], dev(z, y, inj_x, xhi))
    inj_local = pltpu.make_async_copy(col0, inj_dst, inj_recv.at[core])

    @pl.when(inj_self)
    def _():
        inj_local.start()

    @pl.when(jnp.logical_not(inj_self))
    def _():
        inj.start()

    w_copy = remote(col0, w.at[core], w_send.at[0], w_recv.at[0], sibling)
    w_copy.start()
    w_local = pltpu.make_async_copy(col0, w.at[core], loc.at[0])
    w_local.start()

    def spread(which, first, count):
        @pl.when(match)
        def _():
            for u in range(first, first + count):
                pltpu.make_async_copy(
                    abuf.at[u, n // 2, core], abuf.at[u, n // 2, core], sc_recv.at[u]
                ).wait()
            piece = abuf.at[pl.ds(first, count), n // 2, core]

            def one(i, _):
                other = (n + i) % 32
                remote(piece, piece, ag_send.at[which], ag_recv.at[which], dev(other // 4, other % 4, x, core)).start()
                return 0

            lax.fori_loop(1, 32, one, 0)

    spread(0, 0, 1)
    spread(1, 1, 2)

    def bytes_wait(sem, pieces):
        ref = m.at[0 : 8 * pieces, 0:BS]
        pltpu.make_async_copy(ref, ref, sem).wait()

    def sib_copy(which, first, count):
        half = abuf.at[pl.ds(first, count), :, core]
        return remote(half, half, sib_send.at[which], sib_recv.at[which], sibling)

    def lead_half(which, first, count):
        @pl.when(match)
        def _():
            bytes_wait(ag_recv.at[which], 15 * count)

        @pl.when(jnp.logical_not(match))
        def _():
            bytes_wait(ag_recv.at[which], 16 * count)

        sib_copy(which, first, count).start()

    zp = (z + 8 - 4 * xlo) % 8
    near = zp < 4
    far = jnp.logical_not(near)
    zd = (zp, (11 - zp) % 8)
    base = tuple(jnp.where(v < 4, v, 3) for v in zd)
    nsend = tuple(jnp.where((v <= 2) | (v == 7), 3, 4) for v in zd)
    zto = (dev((z + 1) % 8, y, x, core), dev((z + 7) % 8, y, x, core))
    yup = dev(z, (y + 1) % 4, x, core)
    ydown = dev(z, (y + 3) % 4, x, core)
    yto = (yup, ydown)
    yfrom = ((y + 3) % 4, (y + 1) % 4)

    def lag(v):
        return jnp.where(v < 4, 0, 2 * (v - 3))

    lags = tuple(lag(v) for v in zd)

    def source_z(d, q):
        s = (base[d] + 4 - q) % 4
        return s if d == 0 else 3 - s

    def part(zs, ys, first, rows):
        start = (zs * 4 + ys) * BS + first
        return g.at[pl.ds(pl.multiple_of(start, 8), rows), :]

    def zpart(d, q, j, ys):
        return part(source_z(d, q), ys, 2 * ZROWS * d + ZROWS * j, ZROWS)

    def ypart(d, zs, ys):
        return part(zs, ys, YBASE + YROWS * d, YROWS)

    def zcopy(d, q, j, ref):
        return remote(ref, ref, z_send.at[d, q, j], z_recv.at[d, q, j], zto[d])

    def yz_copy(d, q, j, s, ref, to):
        return remote(ref, ref, yz_send.at[d, q, j, s], yz_recv.at[d, q, j, s], to)

    def yy_copy(d, s, ref, to):
        return remote(ref, ref, yy_send.at[d, s], yy_recv.at[d, s], to)

    def near_start():
        @pl.when(near)
        def _():
            for h in range(2):
                pltpu.make_async_copy(col0, col0, inj_recv.at[h]).wait()
            for d in range(2):
                ref = ypart(d, z % 4, y)
                yy_copy(d, 0, ref, yup).start()
                yy_copy(d, 1, ref, ydown).start()

    def near_forward():
        @pl.when(near)
        def _():
            for d in range(2):
                ref = ypart(d, z % 4, yfrom[d])
                yy_copy(d, d, ref, yto[d]).wait_recv()
                yy_copy(d, 2, ref, yto[d]).start()

    def pass_on(d, q, j, ref):
        @pl.when(far | (q > 0))
        def _():
            arrived = jnp.where(near, q - 1, q)
            pltpu.make_async_copy(ref, ref, z_recv.at[d, jnp.maximum(arrived, 0), j]).wait()

        @pl.when(q < nsend[d])
        def _():
            zcopy(d, q, j, ref).start()

    def event(d, e):
        q = e // 6
        j = e % 6

        @pl.when(j < 2)
        def _():
            ref = zpart(d, q, j, y)
            pass_on(d, q, j, ref)
            yz_copy(d, q, j, 0, ref, yup).start()
            yz_copy(d, q, j, 1, ref, ydown).start()

        @pl.when(j >= 2)
        def _():
            i = j - 2
            gray = i + i // 2 - 2 * (i // 3)
            ref = ypart(d, source_z(d, q), (y + gray) % 4)

            for num, s in ((1, 1), (2, 0), (3, 2)):
                if s != d:
                    @pl.when(near & (q == 0) & (i == num))
                    def _():
                        pltpu.make_async_copy(ref, ref, yy_recv.at[d, s]).wait()

            pass_on(d, q, j, ref)

        @pl.when((j == 3) | (j == 4))
        def _():
            ref = zpart(d, q, j - 3, yfrom[d])
            yz_copy(d, q, j - 3, d, ref, yto[d]).wait_recv()
            yz_copy(d, q, j - 3, 2, ref, yto[d]).start()

    def slot(t):
        for d in range(2):
            late = jnp.where(t < 6, t, jnp.where(t < 10, -1, t - 4))
            e = jnp.where(zd[d] == 0, late, t - lags[d])

            @pl.when((e >= 0) & (e < EVENTS))
            def _():
                event(d, e)

        @pl.when(t == 2)
        def _():
            near_forward()

    def finish():
        inj_wait = jnp.logical_not(inj_self)

        @pl.when(inj_wait)
        def _():
            inj.wait_send()

        w_copy.wait_send()

        @pl.when(is_src)
        def _():
            @pl.when(own_src)
            def _():
                bytes_wait(sc_send.at[0], 63)

            @pl.when(jnp.logical_not(own_src))
            def _():
                bytes_wait(sc_send.at[0], 64)

        @pl.when(match)
        def _():
            bytes_wait(ag_send.at[0], 31)
            bytes_wait(ag_send.at[1], 62)

        for which, first, count in ((0, 0, 1), (1, 1, 2)):
            sib_copy(which, first, count).wait_send()

        @pl.when(near)
        def _():
            for d in range(2):
                for s in range(3):
                    yy_copy(d, s, ypart(d, z % 4, y), yup).wait_send()

        def each(q, _):
            for d in range(2):
                for j in range(2):
                    for s in range(3):
                        copy = yz_copy(d, q, j, s, zpart(d, q, j, y), yup)
                        copy.wait_send()
                        if s != d:
                            copy.wait_recv()

                @pl.when(q < nsend[d])
                def _():
                    for j in range(6):
                        ref = zpart(d, q, j, y) if j < 2 else ypart(d, source_z(d, q), y)
                        zcopy(d, q, j, ref).wait_send()
            return 0

        lax.fori_loop(0, 4, each, 0)

    near_start()

    lax.fori_loop(0, SLOTS, lambda t, _: (slot(t), 0)[1], 0)

    eye = (
        lax.broadcasted_iota(jnp.int32, (LEAD, LEAD), 0)
        == lax.broadcasted_iota(jnp.int32, (LEAD, LEAD), 1)
    ).astype(jnp.float32)
    m[:, LEAD:] = eye
    lead_half(0, 0, 1)
    lead_half(1, 1, 2)
    for which, first, count in ((0, 0, 1), (1, 1, 2)):
        sib_copy(which, first, count).wait_recv()
    m[0:BS, 0:BS] = abuf[0].reshape(BS, BS)
    m[0:BS, BS:LEAD] = abuf[1].reshape(BS, BS)
    m[BS:LEAD, BS:LEAD] = abuf[2].reshape(BS, BS)
    m[BS:LEAD, 0:BS] = jnp.zeros((BS, BS), jnp.float32)

    def step(k, _):
        off = pl.multiple_of(k * NB, NB)
        dx[:, 0:NB] = m[pl.ds(off, NB), pl.ds(off, NB)]
        dx[:, NB : 2 * NB] = eye[0:NB, 0:NB]
        diag_factor(dx, lambda p: None)
        mk = dotf(dx[:, NB : 2 * NB], m[pl.ds(off, NB), :], 1, 0)
        m[pl.ds(off, NB), :] = mk

        def trail(i, _):
            oi = pl.multiple_of(i * NB, NB)
            u = m[pl.ds(off, NB), pl.ds(oi, NB)]
            m[pl.ds(oi, NB), :] = m[pl.ds(oi, NB), :] - dotf(u, mk, 0, 0)
            return 0

        lax.fori_loop(k + 1, LEAD // NB, trail, 0)
        return 0

    lax.fori_loop(0, LEAD // NB, step, 0)

    w_copy.wait_recv()
    w_local.wait()
    p0 = dotf(w[0], m[0:BS, LEAD : LEAD + BS], 1, 1)
    p1 = dotf(w[0], m[BS:LEAD, LEAD : LEAD + BS], 1, 1) + dotf(w[1], m[BS:LEAD, LEAD + BS :], 1, 1)
    q_out[:, 0:BS] = dotf(p0, m[0:BS, LEAD : LEAD + BS], 1, 0) + dotf(p1, m[BS:LEAD, LEAD : LEAD + BS], 1, 0)
    q_out[:, BS:LEAD] = dotf(p1, m[BS:LEAD, LEAD + BS :], 1, 0)
    p_out[...] = jnp.where(core == 0, p0, p1)
    ri = lax.broadcasted_iota(jnp.int32, (BS, BS), 0)
    ci = lax.broadcasted_iota(jnp.int32, (BS, BS), 1)

    @pl.when((row == 0) & (core == 0))
    def _():
        p_out[...] = jnp.where(ri >= ci, m[0:BS, 0:BS].T, 0.0)

    @pl.when((row == 0) & (core == 1))
    def _():
        p_out[...] = jnp.zeros((BS, BS), jnp.float32)

    @pl.when((row == 1) & (core == 0))
    def _():
        p_out[...] = m[0:BS, BS:LEAD].T

    @pl.when((row == 1) & (core == 1))
    def _():
        p_out[...] = jnp.where(ri >= ci, m[BS:LEAD, BS:LEAD].T, 0.0)

    finish()


def gather_and_factor(col0):
    dma = pltpu.SemaphoreType.DMA
    vmem = pl.BlockSpec(memory_space=pltpu.VMEM)
    return pl.pallas_call(
        gather_kernel,
        out_shape=(
            jax.ShapeDtypeStruct((16 * BS, LEAD), jnp.float32),
            jax.ShapeDtypeStruct((BS, LEAD), jnp.float32),
            jax.ShapeDtypeStruct((BS, BS), jnp.float32),
        ),
        in_specs=[vmem],
        out_specs=(pl.BlockSpec(memory_space=pl.ANY), vmem, vmem),
        scratch_shapes=[
            pltpu.VMEM((2, BS, BS), jnp.float32),
            pltpu.VMEM((3, 16, 2, 8, BS), jnp.float32),
            pltpu.VMEM((LEAD, 2 * LEAD), jnp.float32),
            pltpu.VMEM((NB, 2 * NB), jnp.float32),
            dma((1,)), dma((2,)), dma((1,)), dma((1,)),
            dma((1,)), dma((3,)), dma((2,)), dma((2,)), dma((2,)), dma((2,)),
            dma((2, 4, 6)), dma((2, 4, 6)), dma((2, 4, 2, 3)), dma((2, 4, 2, 3)), dma((2, 3)), dma((2, 3)),
            dma((1,)),
        ],
        compiler_params=pltpu.CompilerParams(has_side_effects=True, vmem_limit_bytes=40 << 20),
        cost_estimate=pl.CostEstimate(flops=2 * LEAD**3, bytes_accessed=16 << 20, transcendentals=LEAD),
    )(col0)


def update_kernel(layer, base, g, q, panel, out):
    step = pl.program_id(0)
    for b in range(4):
        upd = dotf(q[...], g[b * BS : (b + 1) * BS, :], 1, 1)
        for h in range(2):
            s = 2 * b + h
            out[:, s, :] = base[:, s, :] - upd[:, h * 128 : (h + 1) * 128]

    @pl.when((step == 0) & (layer[0] == 0))
    def _():
        for h in range(2):
            out[:, h, :] = panel[:, h * 128 : (h + 1) * 128]


def update(layer, tile, g, q, panel):
    return pl.pallas_call(
        update_kernel,
        out_shape=jax.ShapeDtypeStruct((BS, 32, 128), jnp.float32),
        grid_spec=pltpu.PrefetchScalarGridSpec(
            num_scalar_prefetch=1,
            grid=(4,),
            in_specs=[
                pl.BlockSpec((BS, 8, 128), lambda i, lay: (0, lay[0] * 4 + i, 0)),
                pl.BlockSpec((4 * BS, LEAD), lambda i, lay: (i, 0)),
                pl.BlockSpec((BS, LEAD), lambda i, lay: (0, 0)),
                pl.BlockSpec((BS, BS), lambda i, lay: (0, 0)),
            ],
            out_specs=pl.BlockSpec((BS, 8, 128), lambda i, lay: (0, i, 0)),
        ),
        compiler_params=pltpu.CompilerParams(vmem_limit_bytes=40 << 20),
        cost_estimate=pl.CostEstimate(flops=2 * BS * LEAD * 16 * BS, bytes_accessed=16 << 20, transcendentals=0),
    )(layer, tile, g, q, panel)


def on_device(matrix):
    tile = matrix.reshape(BS, 64, 128)
    col0 = tile[:, 0:2, :].reshape(BS, BS)
    g, q, panel = gather_and_factor(col0)
    layer = lax.axis_index("layer").reshape(1).astype(jnp.int32)
    out = update(layer, tile, g, q, panel)
    return out.reshape(1, 1, BS, 16, 1, BS)


def solution(mesh):
    in_specs = (P(None, "row", None, None, "col", None),)
    out_specs = P(None, "row", None, "layer", "col", None)
    return jax.shard_map(
        on_device, mesh=mesh, in_specs=in_specs, out_specs=out_specs, check_vma=False
    )
```

```python
import jax
import jax.numpy as jnp
from jax import lax
from jax.experimental import pallas as pl
from jax.experimental.pallas import tpu as pltpu
from jax.sharding import PartitionSpec as P

HIGH = lax.Precision.HIGHEST
BS = 256
LEAD = 2 * BS
NB = 128
ZROWS = 40
YROWS = 48
YBASE = 2 * ZROWS
EVENTS = 24
PIECE = 16
SLOTS = 32
FIRST = 4
MESH = pl.DeviceIdType.MESH


def dotf(a, b, ca, cb):
    return lax.dot_general(
        a, b, (((ca,), (cb,)), ((), ())), precision=HIGH, preferred_element_type=jnp.float32
    )


def diag_factor(dx, between):
    sub = lax.broadcasted_iota(jnp.int32, (8, NB), 0)
    for p in range(NB // 8):
        lo = 8 * p
        left = dx[lo : lo + 8, 0:NB]
        right = dx[lo : lo + 8, NB : 2 * NB]
        cols = [jnp.broadcast_to(left[:, lo + i : lo + i + 1], (8, NB)) for i in range(8)]
        for i in range(8):
            pivot = jnp.broadcast_to(cols[i][i : i + 1, :], (8, NB))
            root = lax.rsqrt(pivot)
            keep = jnp.where(sub == i, root, 1.0)
            mult = jnp.where(sub > i, cols[i] * (root * root), 0.0)
            for k in range(i + 1, 8):
                row = jnp.broadcast_to(cols[k][i : i + 1, :], (8, NB))
                cols[k] = cols[k] * keep - mult * row
            left = left * keep - mult * jnp.broadcast_to(left[i : i + 1, :], (8, NB))
            right = right * keep - mult * jnp.broadcast_to(right[i : i + 1, :], (8, NB))
        both = jnp.concatenate([left, right], axis=1)
        dx[lo : lo + 8, :] = both
        if p < NB // 8 - 1:
            upd = dotf(left, both, 0, 0)
            dx[lo + 8 :, :] = dx[lo + 8 :, :] - upd[lo + 8 :, :]
        between(p)


def gather_kernel(
    col0, tile, out, g, q_out, p_out, w, abuf, m, dx,
    inj_send, inj_recv, w_send, w_recv,
    sc_send, sc_recv, ag_send, ag_recv, sib_send, sib_recv,
    z_send, z_recv, yz_send, yz_recv, yy_send, yy_recv, loc,
):
    row = lax.axis_index("row")
    core = lax.axis_index("col")
    xlo = lax.axis_index("layer")
    z = row // 8
    y = (row // 2) % 4
    xhi = row % 2
    x = xhi * 2 + xlo
    n = z * 4 + y

    def dev(dz, dy, dx_, dc):
        return {"row": dz * 8 + dy * 2 + dx_ // 2, "col": dc, "layer": dx_ % 2}

    def remote(src, dst, ss, rs, to):
        return pltpu.make_async_remote_copy(
            src_ref=src, dst_ref=dst, send_sem=ss, recv_sem=rs, device_id=to, device_id_type=MESH
        )

    sibling = dev(z, y, x, 1 - core)

    unit = xhi + core
    is_src = (row < 2) & ((xhi == 0) | (core == 1))
    own_src = (row == 0) & (core == 0)
    match = (n % 2 == 0) & ((n // 2) % 2 == core)
    zhalf = z // 4
    same = xlo == zhalf
    ring = (
        dev((z + 1) % 8, y, x, core),
        dev((z + 7) % 8, y, x, core),
        dev(z, (y + 1) % 4, x, core),
        dev(z, (y + 3) % 4, x, core),
    )

    barrier = pltpu.get_barrier_semaphore()

    def greet(to):
        pl.semaphore_signal(barrier, inc=1, device_id=to, device_id_type=MESH)

    for to in ring + (sibling,):
        greet(to)

    @pl.when(match)
    def _():
        low = jnp.where(xhi == 0, x, 3 - x)

        @pl.when(jnp.logical_not(own_src))
        def _():
            greet(dev(0, 0, low, 0))

        greet(dev(0, 0, low, 1))
        greet(dev(0, 0, 3 - low, 1))

    @pl.when(same & (core != xhi))
    def _():
        greet(dev(z, y, 3 - x, 0))
        greet(dev(z, y, 3 - x, 1))

    def greet_holder(i, _):
        holder = 4 * i + 2 * core

        @pl.when(holder != n)
        def _():
            greet(dev(holder // 4, holder % 4, x, core))

        return 0

    lax.fori_loop(0, 8, greet_holder, 0)
    pl.semaphore_wait(
        barrier,
        5
        + jnp.where(match, 31, 0)
        + jnp.where(is_src, 32, 0)
        - jnp.where(own_src, 1, 0)
        + jnp.where(same, 0, 1),
    )

    @pl.when(is_src)
    def _():
        for i in range(16):
            src = col0.at[PIECE * i : PIECE * (i + 1), :]
            dst = abuf.at[unit, i // 2, i % 2]
            hz, hy = i // 2, 2 * (i % 2)
            here = remote(src, dst, sc_send.at[0], sc_recv.at[unit], dev(hz, hy, x, i % 2))
            if i == 0:
                @pl.when(own_src)
                def _():
                    pltpu.make_async_copy(src, dst, sc_recv.at[unit]).start()

                @pl.when(jnp.logical_not(own_src))
                def _():
                    here.start()
            else:
                here.start()
            remote(src, dst, sc_send.at[0], sc_recv.at[unit], dev(hz, hy, 3 - x, i % 2)).start()

    inj_x = jnp.where(same, x, 3 - x)
    inj_self = same & (xhi == core)
    own_slot = (z % 4) * 4 + y
    inj_dst = g.at[pl.ds(pl.multiple_of(own_slot * BS, BS), BS), pl.ds(pl.multiple_of(core * BS, BS), BS)]
    inj = remote(col0, inj_dst, inj_send.at[0], inj_recv.at[core], dev(z, y, inj_x, xhi))
    inj_local = pltpu.make_async_copy(col0, inj_dst, inj_recv.at[core])

    @pl.when(inj_self)
    def _():
        inj_local.start()

    @pl.when(jnp.logical_not(inj_self))
    def _():
        inj.start()

    w_copy = remote(col0, w.at[core], w_send.at[0], w_recv.at[0], sibling)
    w_copy.start()
    w_local = pltpu.make_async_copy(col0, w.at[core], loc.at[0])
    w_local.start()
    tile_copy = pltpu.make_async_copy(tile.at[:, pl.ds(pl.multiple_of(xlo * 32, 32), 32), :], out, loc.at[1])
    tile_copy.start()

    def spread(which, first, count):
        @pl.when(match)
        def _():
            for u in range(first, first + count):
                pltpu.make_async_copy(
                    abuf.at[u, n // 4, core], abuf.at[u, n // 4, core], sc_recv.at[u]
                ).wait()
            piece = abuf.at[pl.ds(first, count), n // 4, core]

            def one(i, _):
                other = (n + i) % 32
                remote(piece, piece, ag_send.at[which], ag_recv.at[which], dev(other // 4, other % 4, x, core)).start()
                return 0

            lax.fori_loop(1, 32, one, 0)


    def bytes_wait(sem, pieces):
        ref = m.at[0 : 8 * pieces, 0:LEAD]
        pltpu.make_async_copy(ref, ref, sem).wait()

    def sib_copy(which, first, count):
        half = abuf.at[pl.ds(first, count), :, core]
        return remote(half, half, sib_send.at[which], sib_recv.at[which], sibling)

    def lead_half(which, first, count):
        @pl.when(match)
        def _():
            bytes_wait(ag_recv.at[which], 7 * count)

        @pl.when(jnp.logical_not(match))
        def _():
            bytes_wait(ag_recv.at[which], 8 * count)

        sib_copy(which, first, count).start()

    zp = (z + 8 - 4 * xlo) % 8
    near = zp < 4
    far = jnp.logical_not(near)
    zd = (zp, (11 - zp) % 8)
    base = tuple(jnp.where(v < 4, v, 3) for v in zd)
    nsend = tuple(jnp.where((v <= 2) | (v == 7), 3, 4) for v in zd)
    zto = (dev((z + 1) % 8, y, x, core), dev((z + 7) % 8, y, x, core))
    yup = dev(z, (y + 1) % 4, x, core)
    ydown = dev(z, (y + 3) % 4, x, core)
    yto = (yup, ydown)
    yfrom = ((y + 3) % 4, (y + 1) % 4)

    def lag(v):
        return jnp.where(v < 4, 0, 2 * (v - 3))

    lags = tuple(lag(v) for v in zd)

    def source_z(d, q):
        s = (base[d] + 4 - q) % 4
        return s if d == 0 else 3 - s

    def part(zs, ys, first, rows):
        start = (zs * 4 + ys) * BS + first
        return g.at[pl.ds(pl.multiple_of(start, 8), rows), :]

    def zpart(d, q, j, ys):
        return part(source_z(d, q), ys, NB * d + ZROWS * j, ZROWS)

    def ypart(d, zs, ys):
        return part(zs, ys, NB * d + YBASE, YROWS)

    def zcopy(d, q, j, ref):
        return remote(ref, ref, z_send.at[d, q, j], z_recv.at[d, q, j], zto[d])

    def yz_copy(d, q, j, s, ref, to):
        return remote(ref, ref, yz_send.at[d, q, j, s], yz_recv.at[d, q, j, s], to)

    def yy_copy(d, s, ref, to):
        return remote(ref, ref, yy_send.at[d, s], yy_recv.at[d, s], to)

    def near_start():
        @pl.when(near)
        def _():
            for h in range(2):
                pltpu.make_async_copy(col0, col0, inj_recv.at[h]).wait()
            for d in range(2):
                ref = ypart(d, z % 4, y)
                yy_copy(d, 0, ref, yup).start()
                yy_copy(d, 1, ref, ydown).start()

    def near_forward():
        @pl.when(near)
        def _():
            for d in range(2):
                ref = ypart(d, z % 4, yfrom[d])
                yy_copy(d, d, ref, yto[d]).wait_recv()
                yy_copy(d, 2, ref, yto[d]).start()

    def pass_on(d, q, j, ref):
        @pl.when(far | (q > 0))
        def _():
            arrived = jnp.where(near, q - 1, q)
            pltpu.make_async_copy(ref, ref, z_recv.at[d, jnp.maximum(arrived, 0), j]).wait()

        @pl.when(q < nsend[d])
        def _():
            zcopy(d, q, j, ref).start()

    def event(d, e):
        q = e // 6
        j = e % 6

        @pl.when(j < 2)
        def _():
            ref = zpart(d, q, j, y)
            pass_on(d, q, j, ref)
            yz_copy(d, q, j, 0, ref, yup).start()
            yz_copy(d, q, j, 1, ref, ydown).start()

        @pl.when(j >= 2)
        def _():
            i = j - 2
            gray = i + i // 2 - 2 * (i // 3)
            ref = ypart(d, source_z(d, q), (y + gray) % 4)

            for num, s in ((1, 1), (2, 0), (3, 2)):
                if s != d:
                    @pl.when(near & (q == 0) & (i == num))
                    def _():
                        pltpu.make_async_copy(ref, ref, yy_recv.at[d, s]).wait()

            pass_on(d, q, j, ref)

        @pl.when((j == 3) | (j == 4))
        def _():
            ref = zpart(d, q, j - 3, yfrom[d])
            yz_copy(d, q, j - 3, d, ref, yto[d]).wait_recv()
            yz_copy(d, q, j - 3, 2, ref, yto[d]).start()

    def slot(t):
        t = jnp.int32(t)
        for d in range(2):
            late = jnp.where(t < 6, t, jnp.where(t < 10, -1, t - 4))
            e = jnp.where(zd[d] == 0, late, t - lags[d])

            @pl.when((e >= 0) & (e < EVENTS))
            def _():
                event(d, e)

        @pl.when(jnp.int32(t) == 2)
        def _():
            near_forward()

    def finish():
        inj_wait = jnp.logical_not(inj_self)

        @pl.when(inj_wait)
        def _():
            inj.wait_send()

        w_copy.wait_send()

        @pl.when(is_src)
        def _():
            @pl.when(own_src)
            def _():
                bytes_wait(sc_send.at[0], 31)

            @pl.when(jnp.logical_not(own_src))
            def _():
                bytes_wait(sc_send.at[0], 32)

        @pl.when(match)
        def _():
            bytes_wait(ag_send.at[0], 31)
            bytes_wait(ag_send.at[1], 62)

        for which, first, count in ((0, 0, 1), (1, 1, 2)):
            sib_copy(which, first, count).wait_send()

        @pl.when(near)
        def _():
            for d in range(2):
                for s in range(3):
                    yy_copy(d, s, ypart(d, z % 4, y), yup).wait_send()

        def each(q, _):
            for d in range(2):
                for j in range(2):
                    for s in range(3):
                        copy = yz_copy(d, q, j, s, zpart(d, q, j, y), yup)
                        copy.wait_send()

                @pl.when(q < nsend[d])
                def _():
                    for j in range(6):
                        ref = zpart(d, q, j, y) if j < 2 else ypart(d, source_z(d, q), y)
                        zcopy(d, q, j, ref).wait_send()
            return 0

        lax.fori_loop(0, 4, each, 0)

    near_start()
    slot(0)
    spread(0, 0, 1)
    spread(1, 1, 2)
    slot(1)
    lead_half(0, 0, 1)
    slot(2)
    lead_half(1, 1, 2)
    slot(3)

    eye = (
        lax.broadcasted_iota(jnp.int32, (LEAD, LEAD), 0)
        == lax.broadcasted_iota(jnp.int32, (LEAD, LEAD), 1)
    ).astype(jnp.float32)
    m[:, LEAD:] = eye
    sib_copy(0, 0, 1).wait_recv()
    m[0:BS, 0:BS] = abuf[0].reshape(BS, BS)
    m[BS:LEAD, 0:BS] = jnp.zeros((BS, BS), jnp.float32)

    def step(k, _):
        off = pl.multiple_of(k * NB, NB)
        dx[:, 0:NB] = m[pl.ds(off, NB), pl.ds(off, NB)]
        dx[:, NB : 2 * NB] = eye[0:NB, 0:NB]

        def between(p):
            if p % 3 == 0 and p < 15:
                slot(FIRST + 5 * k + p // 3)

        diag_factor(dx, between)

        @pl.when(k == 0)
        def _():
            sib_copy(1, 1, 2).wait_recv()
            m[0:BS, BS:LEAD] = abuf[1].reshape(BS, BS)
            m[BS:LEAD, BS:LEAD] = abuf[2].reshape(BS, BS)

        mk = dotf(dx[:, NB : 2 * NB], m[pl.ds(off, NB), :], 1, 0)
        m[pl.ds(off, NB), :] = mk

        def trail(i, _):
            oi = pl.multiple_of(i * NB, NB)
            u = m[pl.ds(off, NB), pl.ds(oi, NB)]
            m[pl.ds(oi, NB), :] = m[pl.ds(oi, NB), :] - dotf(u, mk, 0, 0)
            return 0

        lax.fori_loop(k + 1, LEAD // NB, trail, 0)
        return 0

    lax.fori_loop(0, LEAD // NB, step, 0)

    slot(FIRST + 20)
    w_copy.wait_recv()
    w_local.wait()
    p0 = dotf(w[0], m[0:BS, LEAD : LEAD + BS], 1, 1)
    p1 = dotf(w[0], m[BS:LEAD, LEAD : LEAD + BS], 1, 1) + dotf(w[1], m[BS:LEAD, LEAD + BS :], 1, 1)
    q_out[:, 0:BS] = dotf(p0, m[0:BS, LEAD : LEAD + BS], 1, 0) + dotf(p1, m[BS:LEAD, LEAD : LEAD + BS], 1, 0)
    q_out[:, BS:LEAD] = dotf(p1, m[BS:LEAD, LEAD + BS :], 1, 0)
    slot(FIRST + 21)
    p_out[...] = jnp.where(core == 0, p0, p1)
    ri = lax.broadcasted_iota(jnp.int32, (BS, BS), 0)
    ci = lax.broadcasted_iota(jnp.int32, (BS, BS), 1)

    @pl.when((row == 0) & (core == 0))
    def _():
        p_out[...] = jnp.where(ri >= ci, m[0:BS, 0:BS].T, 0.0)

    @pl.when((row == 0) & (core == 1))
    def _():
        p_out[...] = jnp.zeros((BS, BS), jnp.float32)

    @pl.when((row == 1) & (core == 0))
    def _():
        p_out[...] = m[0:BS, BS:LEAD].T

    @pl.when((row == 1) & (core == 1))
    def _():
        p_out[...] = jnp.where(ri >= ci, m[BS:LEAD, BS:LEAD].T, 0.0)

    tile_copy.wait()
    flat = out.reshape(BS * 32, NB)

    def work(i, _):
        q = i // 2

        @pl.when(i % 2 == 0)
        def _():
            for d in range(2):
                for j in range(2):
                    for s in range(3):
                        if s != d:
                            yz_copy(d, q, j, s, zpart(d, q, j, y), yup).wait_recv()

        for d in range(2):
            ids = [(source_z(d, q) * 4 + 2 * (i % 2) + h) * 2 + d for h in range(2)]
            rows = [g[pl.ds(pl.multiple_of(v * NB, NB), NB), :] for v in ids]
            upd = dotf(q_out[...], jnp.concatenate(rows, axis=0), 1, 1)
            for h in range(2):
                where = pl.ds(ids[h], BS, stride=32)
                flat[where, :] = flat[where, :] - upd[:, h * NB : (h + 1) * NB]
        return 0

    def slot_and_work(i, _):
        slot(FIRST + 22 + i)
        return work(i, 0)

    lax.fori_loop(0, 6, slot_and_work, 0)
    lax.fori_loop(6, 8, work, 0)

    @pl.when(xlo == 0)
    def _():
        for h in range(2):
            out[:, h, :] = p_out[:, h * NB : (h + 1) * NB]

    finish()


def factor_and_update(col0, tile):
    dma = pltpu.SemaphoreType.DMA
    vmem = pl.BlockSpec(memory_space=pltpu.VMEM)
    return pl.pallas_call(
        gather_kernel,
        out_shape=jax.ShapeDtypeStruct((BS, 32, NB), jnp.float32),
        in_specs=[vmem, pl.BlockSpec(memory_space=pl.ANY)],
        out_specs=vmem,
        scratch_shapes=[
            pltpu.VMEM((16 * BS, LEAD), jnp.float32),
            pltpu.VMEM((BS, LEAD), jnp.float32),
            pltpu.VMEM((BS, BS), jnp.float32),
            pltpu.VMEM((2, BS, BS), jnp.float32),
            pltpu.VMEM((3, 8, 2, PIECE, BS), jnp.float32),
            pltpu.VMEM((LEAD, 2 * LEAD), jnp.float32),
            pltpu.VMEM((NB, 2 * NB), jnp.float32),
            dma((1,)), dma((2,)), dma((1,)), dma((1,)),
            dma((1,)), dma((3,)), dma((2,)), dma((2,)), dma((2,)), dma((2,)),
            dma((2, 4, 6)), dma((2, 4, 6)), dma((2, 4, 2, 3)), dma((2, 4, 2, 3)), dma((2, 3)), dma((2, 3)),
            dma((2,)),
        ],
        compiler_params=pltpu.CompilerParams(
            has_side_effects=True, collective_id=0, vmem_limit_bytes=46 << 20
        ),
        cost_estimate=pl.CostEstimate(
            flops=2 * BS * LEAD * 16 * BS, bytes_accessed=16 << 20, transcendentals=LEAD
        ),
    )(col0, tile)


def on_device(matrix):
    tile = matrix.reshape(BS, 64, NB)
    col0 = tile[:, 0:2, :].reshape(BS, BS)
    return factor_and_update(col0, tile).reshape(1, 1, BS, 16, 1, BS)


def solution(mesh):
    in_specs = (P(None, "row", None, None, "col", None),)
    out_specs = P(None, "row", None, "layer", "col", None)
    return jax.shard_map(
        on_device, mesh=mesh, in_specs=in_specs, out_specs=out_specs, check_vma=False
    )
```

```python
import jax
import jax.numpy as jnp
from jax import lax
from jax.experimental import pallas as pl
from jax.experimental.pallas import tpu as pltpu
from jax.sharding import PartitionSpec as P

HIGH = lax.Precision.HIGHEST
BS = 256
LEAD = 2 * BS
NB = 128
ZROWS = 40
YROWS = 48
YBASE = 2 * ZROWS
EVENTS = 24
PIECE = 16
YWAIT = ((1, 2), (0, 2))
LAG = 3
SLOTS = EVENTS + 4 * LAG
FIRST = 4
MESH = pl.DeviceIdType.MESH


def dotf(a, b, ca, cb):
    return lax.dot_general(
        a, b, (((ca,), (cb,)), ((), ())), precision=HIGH, preferred_element_type=jnp.float32
    )


def parts(v):
    high = v.astype(jnp.bfloat16).astype(jnp.float32)
    rest = v - high
    mid = rest.astype(jnp.bfloat16).astype(jnp.float32)
    low = (rest - mid).astype(jnp.bfloat16).astype(jnp.float32)
    return high, mid, low


def rank8(left, both):
    a, b, c = parts(left)
    d, e, f = parts(both)
    return lax.dot_general(
        jnp.concatenate([a, a, b, a, c, b], axis=0),
        jnp.concatenate([d, e, d, f, d, e], axis=0),
        (((0,), (0,)), ((), ())),
        preferred_element_type=jnp.float32,
    )


def down(v, i):
    return jnp.broadcast_to(v[i : i + 1, :], (8, NB))


def across(v, j):
    return jnp.broadcast_to(v[:, j : j + 1], (8, NB))


def diag_factor(dx, between):
    sub = lax.broadcasted_iota(jnp.int32, (8, NB), 0)
    left = dx[0:8, 0:NB]
    right = dx[0:8, NB : 2 * NB]
    for p in range(NB // 8):
        lo = 8 * p
        ahead = p < NB // 8 - 1
        cols = [across(left, lo + i) for i in range(8)]
        if ahead:
            left2 = dx[lo + 8 : lo + 16, 0:NB]
            right2 = dx[lo + 8 : lo + 16, NB : 2 * NB]
            cols2 = [across(left2, lo + i) for i in range(8)]
        scale = None
        for i in range(8):
            root = lax.rsqrt(down(cols[i], i))
            inv = root * root
            scale = root if scale is None else jnp.where(sub == i, root, scale)
            below = jnp.where(sub > i, cols[i], 0.0)
            for k in range(i + 1, 8):
                row = down(cols[k], i) * inv
                cols[k] = cols[k] - below * row
                if ahead:
                    cols2[k] = cols2[k] - cols2[i] * row
            row_l = down(left, i) * inv
            row_r = down(right, i) * inv
            left = left - below * row_l
            right = right - below * row_r
            if ahead:
                left2 = left2 - cols2[i] * row_l
                right2 = right2 - cols2[i] * row_r
        left = left * scale
        both = jnp.concatenate([left, right * scale], axis=1)
        dx[lo : lo + 8, :] = both
        if lo + 16 < NB:
            upd = rank8(left, both)
            dx[lo + 16 :, :] = dx[lo + 16 :, :] - upd[lo + 16 :, :]
        if ahead:
            left, right = left2, right2
        between(p)


def gather_kernel(
    col0, tile, out, g, q_out, p_out, w, abuf, m, dx, raw, own,
    inj_send, inj_recv, w_send, w_recv,
    sc_send, sc_recv, ag_send, ag_recv, sib_send, sib_recv,
    z_send, z_recv, yz_send, yz_recv, yy_send, yy_recv, x_send, x_recv, loc,
):
    row = lax.axis_index("row")
    core = lax.axis_index("col")
    xlo = lax.axis_index("layer")
    z = row // 8
    y = (row // 2) % 4
    xhi = row % 2
    x = xhi * 2 + xlo
    n = z * 4 + y

    def dev(dz, dy, dx_, dc):
        high = jnp.where(dx_ >= 2, 1, 0)
        return {"row": dz * 8 + dy * 2 + high, "col": dc, "layer": dx_ - 2 * high}

    def remote(src, dst, ss, rs, to):
        return pltpu.make_async_remote_copy(
            src_ref=src, dst_ref=dst, send_sem=ss, recv_sem=rs, device_id=to, device_id_type=MESH
        )

    sibling = dev(z, y, x, 1 - core)

    unit = xhi + core
    is_src = (row < 2) & ((xhi == 0) | (core == 1))
    own_src = (row == 0) & (core == 0)
    match = (n % 2 == 0) & ((n // 2) % 2 == core)
    zhalf = z // 4
    same = xlo == zhalf
    ring = (
        dev((z + 1) % 8, y, x, core),
        dev((z + 7) % 8, y, x, core),
        dev(z, (y + 1) % 4, x, core),
        dev(z, (y + 3) % 4, x, core),
    )

    barrier = pltpu.get_barrier_semaphore()

    def greet(to):
        pl.semaphore_signal(barrier, inc=1, device_id=to, device_id_type=MESH)

    twin = dev(z, y, (x + 2) % 4, core)
    native = core == xhi
    for to in ring + (sibling, twin):
        greet(to)

    @pl.when(match)
    def _():
        low = jnp.where(xhi == 0, x, 3 - x)

        @pl.when(jnp.logical_not(own_src))
        def _():
            greet(dev(0, 0, low, 0))

        greet(dev(0, 0, low, 1))
        greet(dev(0, 0, 3 - low, 1))

    @pl.when(same & (core != xhi))
    def _():
        greet(dev(z, y, 3 - x, 0))
        greet(dev(z, y, 3 - x, 1))

    def greet_holder(i, _):
        holder = 4 * i + 2 * core

        @pl.when(holder != n)
        def _():
            greet(dev(holder // 4, holder % 4, x, core))

        return 0

    lax.fori_loop(0, 8, greet_holder, 0)
    pl.semaphore_wait(
        barrier,
        6
        + jnp.where(match, 31, 0)
        + jnp.where(is_src, 32, 0)
        - jnp.where(own_src, 1, 0)
        + jnp.where(same, 0, 1),
    )

    @pl.when(is_src)
    def _():
        for i in range(16):
            src = col0.at[PIECE * i : PIECE * (i + 1), :]
            dst = abuf.at[unit, i // 2, i % 2]
            hz, hy = i // 2, 2 * (i % 2)
            here = remote(src, dst, sc_send.at[0], sc_recv.at[unit], dev(hz, hy, x, i % 2))
            if i == 0:
                @pl.when(own_src)
                def _():
                    pltpu.make_async_copy(src, dst, sc_recv.at[unit]).start()

                @pl.when(jnp.logical_not(own_src))
                def _():
                    here.start()
            else:
                here.start()
            remote(src, dst, sc_send.at[0], sc_recv.at[unit], dev(hz, hy, 3 - x, i % 2)).start()

    inj_x = jnp.where(same, x, 3 - x)
    inj_self = same & (xhi == core)
    zown = z % 4
    own_slot = zown * 4 + y
    inj_dst = g.at[pl.ds(pl.multiple_of(own_slot * BS, BS), BS), pl.ds(pl.multiple_of(core * BS, BS), BS)]
    inj = remote(col0, inj_dst, inj_send.at[0], inj_recv.at[core], dev(z, y, inj_x, xhi))
    inj_local = pltpu.make_async_copy(col0, inj_dst, inj_recv.at[core])

    @pl.when(inj_self)
    def _():
        inj_local.start()

    @pl.when(jnp.logical_not(inj_self))
    def _():
        inj.start()

    w_copy = remote(col0, w.at[core], w_send.at[0], w_recv.at[0], sibling)
    w_copy.start()
    w_local = pltpu.make_async_copy(col0, w.at[core], loc.at[0])
    w_local.start()
    tile_copy = pltpu.make_async_copy(tile.at[:, pl.ds(pl.multiple_of(xlo * 32, 32), 32), :], raw, loc.at[1])
    tile_copy.start()

    def spread(which, first, count):
        @pl.when(match)
        def _():
            for u in range(first, first + count):
                pltpu.make_async_copy(
                    abuf.at[u, n // 4, core], abuf.at[u, n // 4, core], sc_recv.at[u]
                ).wait()
            piece = abuf.at[pl.ds(first, count), n // 4, core]

            def one(i, _):
                other = (n + i) % 32
                remote(piece, piece, ag_send.at[which], ag_recv.at[which], dev(other // 4, other % 4, x, core)).start()
                return 0

            lax.fori_loop(1, 32, one, 0)


    def bytes_wait(sem, pieces):
        ref = m.at[0 : 8 * pieces, 0:LEAD]
        pltpu.make_async_copy(ref, ref, sem).wait()

    def sib_copy(which, first, count):
        half = abuf.at[pl.ds(first, count), :, core]
        return remote(half, half, sib_send.at[which], sib_recv.at[which], sibling)

    def lead_half(which, first, count):
        @pl.when(match)
        def _():
            bytes_wait(ag_recv.at[which], 7 * count)

        @pl.when(jnp.logical_not(match))
        def _():
            bytes_wait(ag_recv.at[which], 8 * count)

        sib_copy(which, first, count).start()

    zp = (z + 8 - 4 * xlo) % 8
    near = zp < 4
    far = jnp.logical_not(near)
    zd = (zp, (11 - zp) % 8)
    base = tuple(jnp.where(v < 4, v, 3) for v in zd)
    nsend = tuple(jnp.where((v <= 2) | (v == 7), 3, 4) for v in zd)
    zto = (dev((z + 1) % 8, y, x, core), dev((z + 7) % 8, y, x, core))
    yup = dev(z, (y + 1) % 4, x, core)
    ydown = dev(z, (y + 3) % 4, x, core)
    yto = (yup, ydown)
    yfrom = ((y + 3) % 4, (y + 1) % 4)

    def event_at(v, t):
        turn = 6 * (v + 1)
        late = t - ((5 + v) * LAG - turn)
        wrap = jnp.where(late >= turn, late, -1)
        return jnp.where(v < 4, jnp.where((t < turn) | (v == 3), t, wrap), t - LAG * (v - 3))

    def wrap4(v):
        return jnp.where(v >= 4, v - 4, v)

    def source_z(d, q):
        s = wrap4(base[d] + 4 - q)
        return s if d == 0 else 3 - s

    def part(zs, ys, first, rows):
        start = (zs * 4 + ys) * BS + first
        return g.at[pl.ds(pl.multiple_of(start, 8), rows), :]

    def zpart(d, q, j, ys):
        return part(source_z(d, q), ys, NB * d + ZROWS * j, ZROWS)

    def ypart(d, zs, ys):
        return part(zs, ys, NB * d + YBASE, YROWS)

    def zcopy(d, q, j, ref):
        return remote(ref, ref, z_send.at[d, q, j], z_recv.at[d, q, j], zto[d])

    def yz_copy(d, q, j, s, ref, to):
        return remote(ref, ref, yz_send.at[d, q, j, s], yz_recv.at[d, q, j, s], to)

    def x_copy(d, q, j, ref):
        return remote(ref, ref, x_send.at[d, q, j], x_recv.at[d, q, j], twin)

    def yy_copy(d, s, ref, to):
        return remote(ref, ref, yy_send.at[d, s], yy_recv.at[d, s], to)

    def unpack(first, last):
        if first == 0:
            tile_copy.wait()
        for v in range(first, last):
            own[v] = raw[:, v, :]

    def near_start():
        @pl.when(near)
        def _():
            for h in range(2):
                pltpu.make_async_copy(col0, col0, inj_recv.at[h]).wait()
            for d in range(2):
                ref = ypart(d, zown, y)
                yy_copy(d, 0, ref, yup).start()
                yy_copy(d, 1, ref, ydown).start()

    def near_forward():
        @pl.when(near)
        def _():
            for d in range(2):
                ref = ypart(d, zown, yfrom[d])
                yy_copy(d, d, ref, yto[d]).wait_recv()
                yy_copy(d, 2, ref, yto[d]).start()

    def pass_on(d, q, j, ref):
        @pl.when(far | (q > 0))
        def _():
            arrived = jnp.where(near, q - 1, q)
            pltpu.make_async_copy(ref, ref, z_recv.at[d, jnp.maximum(arrived, 0), j]).wait()

        @pl.when(q < nsend[d])
        def _():
            zcopy(d, q, j, ref).start()

    def event(d, e):
        q = jnp.where(e >= 18, 3, jnp.where(e >= 12, 2, jnp.where(e >= 6, 1, 0)))
        j = e - 6 * q

        @pl.when(j < 2)
        def _():
            ref = zpart(d, q, j, y)
            pass_on(d, q, j, ref)
            yz_copy(d, q, j, 0, ref, yup).start()
            yz_copy(d, q, j, 1, ref, ydown).start()

        @pl.when((j >= 2) & native)
        def _():
            i = j - 2
            gray = jnp.where(i == 2, 3, jnp.where(i == 3, 2, i))
            ref = ypart(d, source_z(d, q), wrap4(y + gray))

            for num, s in ((1, 1), (2, 0), (3, 2)):
                if s != d:
                    @pl.when(near & (q == 0) & (i == num))
                    def _():
                        pltpu.make_async_copy(ref, ref, yy_recv.at[d, s]).wait()

            pass_on(d, q, j, ref)

            @pl.when(far | (q > 0))
            def _():
                x_copy(d, q, i, ref).start()

        @pl.when((j == 3) | (j == 4))
        def _():
            ref = zpart(d, q, j - 3, yfrom[d])
            yz_copy(d, q, j - 3, d, ref, yto[d]).wait_recv()
            yz_copy(d, q, j - 3, 2, ref, yto[d]).start()

    def slot(t):
        t = jnp.int32(t)
        for d in range(2):
            e = event_at(zd[d], t)

            @pl.when((e >= 0) & (e < EVENTS))
            def _():
                event(d, e)

        @pl.when(jnp.int32(t) == 2)
        def _():
            near_forward()

    def finish():
        inj_wait = jnp.logical_not(inj_self)

        @pl.when(inj_wait)
        def _():
            inj.wait_send()

        w_copy.wait_send()

        @pl.when(is_src)
        def _():
            @pl.when(own_src)
            def _():
                bytes_wait(sc_send.at[0], 31)

            @pl.when(jnp.logical_not(own_src))
            def _():
                bytes_wait(sc_send.at[0], 32)

        @pl.when(match)
        def _():
            bytes_wait(ag_send.at[0], 31)
            bytes_wait(ag_send.at[1], 62)

        for which, first, count in ((0, 0, 1), (1, 1, 2)):
            sib_copy(which, first, count).wait_send()

        @pl.when(near)
        def _():
            for d in range(2):
                for s in range(3):
                    yy_copy(d, s, ypart(d, zown, y), yup).wait_send()

        def each(q, _):
            for d in range(2):
                for j in range(2):
                    for s in range(3):
                        copy = yz_copy(d, q, j, s, zpart(d, q, j, y), yup)
                        copy.wait_send()

                @pl.when(q < nsend[d])
                def _():
                    for j in range(2):
                        zcopy(d, q, j, zpart(d, q, j, y)).wait_send()

                @pl.when(native)
                def _():
                    ref = ypart(d, source_z(d, q), y)
                    for j in range(4):
                        @pl.when(q < nsend[d])
                        def _():
                            zcopy(d, q, 2 + j, ref).wait_send()

                        @pl.when(far | (q > 0))
                        def _():
                            x_copy(d, q, j, ref).wait_send()
            return 0

        lax.fori_loop(0, 4, each, 0)

    near_start()
    slot(0)
    spread(0, 0, 1)
    slot(1)
    unpack(0, 16)
    slot(2)
    lead_half(0, 0, 1)
    spread(1, 1, 2)
    slot(3)
    unpack(16, 32)

    eye = (
        lax.broadcasted_iota(jnp.int32, (LEAD, LEAD), 0)
        == lax.broadcasted_iota(jnp.int32, (LEAD, LEAD), 1)
    ).astype(jnp.float32)
    m[:, LEAD:] = eye
    sib_copy(0, 0, 1).wait_recv()
    m[0:BS, 0:BS] = abuf[0].reshape(BS, BS)
    m[BS:LEAD, 0:BS] = jnp.zeros((BS, BS), jnp.float32)

    def step(k, _):
        off = pl.multiple_of(k * NB, NB)
        dx[:, 0:NB] = m[pl.ds(off, NB), pl.ds(off, NB)]
        dx[:, NB : 2 * NB] = eye[0:NB, 0:NB]

        def between(p):
            if p % 3 == 0 and p < 18:
                slot(FIRST + 6 * k + p // 3)
            if p == 8:
                @pl.when(k == 0)
                def _():
                    lead_half(1, 1, 2)

        diag_factor(dx, between)

        @pl.when(k == 0)
        def _():
            sib_copy(1, 1, 2).wait_recv()
            m[0:BS, BS:LEAD] = abuf[1].reshape(BS, BS)
            m[BS:LEAD, BS:LEAD] = abuf[2].reshape(BS, BS)

        span = pl.ds(off, LEAD + NB)
        mk = dotf(dx[:, NB : 2 * NB], m[pl.ds(off, NB), span], 1, 0)
        m[pl.ds(off, NB), span] = mk

        def trail(i, _):
            oi = pl.multiple_of(i * NB, NB)
            u = m[pl.ds(off, NB), pl.ds(oi, NB)]
            m[pl.ds(oi, NB), span] = m[pl.ds(oi, NB), span] - dotf(u, mk, 0, 0)
            return 0

        lax.fori_loop(k + 1, LEAD // NB, trail, 0)
        return 0

    lax.fori_loop(0, LEAD // NB, step, 0)

    slot(28)
    w_copy.wait_recv()
    w_local.wait()
    p0 = dotf(w[0], m[0:BS, LEAD : LEAD + BS], 1, 1)
    p1 = dotf(w[0], m[BS:LEAD, LEAD : LEAD + BS], 1, 1) + dotf(w[1], m[BS:LEAD, LEAD + BS :], 1, 1)
    q_out[:, 0:BS] = dotf(p0, m[0:BS, LEAD : LEAD + BS], 1, 0) + dotf(p1, m[BS:LEAD, LEAD : LEAD + BS], 1, 0)
    q_out[:, BS:LEAD] = dotf(p1, m[BS:LEAD, LEAD + BS :], 1, 0)
    slot(29)
    p_out[...] = jnp.where(core == 0, p0, p1)
    ri = lax.broadcasted_iota(jnp.int32, (BS, BS), 0)
    ci = lax.broadcasted_iota(jnp.int32, (BS, BS), 1)

    @pl.when((row == 0) & (core == 0))
    def _():
        p_out[...] = jnp.where(ri >= ci, m[0:BS, 0:BS].T, 0.0)

    @pl.when((row == 0) & (core == 1))
    def _():
        p_out[...] = jnp.zeros((BS, BS), jnp.float32)

    @pl.when((row == 1) & (core == 0))
    def _():
        p_out[...] = m[0:BS, BS:LEAD].T

    @pl.when((row == 1) & (core == 1))
    def _():
        p_out[...] = jnp.where(ri >= ci, m[BS:LEAD, BS:LEAD].T, 0.0)

    flat = out.reshape(BS * 32, NB)

    def work(i, _):
        q = i // 2

        @pl.when(i % 2 == 0)
        def _():
            for d in range(2):
                for j in range(2):
                    for s in range(3):
                        if s != d:
                            yz_copy(d, q, j, s, zpart(d, q, j, y), yup).wait_recv()

            @pl.when(jnp.logical_not(native))
            def _():
                for d in range(2):
                    for j in range(4):
                        ref = ypart(d, source_z(d, q), y)

                        @pl.when(far | (q > 0))
                        def _():
                            x_copy(d, q, j, ref).wait_recv()

                    for s in YWAIT[d]:
                        @pl.when(near & (q == 0))
                        def _():
                            yy_copy(d, s, ypart(d, zown, y), yup).wait_recv()

        for d in range(2):
            ids = [(source_z(d, q) * 4 + 2 * (i % 2) + h) * 2 + d for h in range(2)]
            rows = [g[pl.ds(pl.multiple_of(v * NB, NB), NB), :] for v in ids]
            upd = dotf(q_out[...], jnp.concatenate(rows, axis=0), 1, 1)
            for h in range(2):
                where = pl.ds(ids[h], BS, stride=32)
                flat[where, :] = own[ids[h]] - upd[:, h * NB : (h + 1) * NB]
        return 0

    def slots(first, last):
        lax.fori_loop(first, last, lambda t, _: (slot(t), 0)[1], 0)

    slots(30, 31)
    lax.fori_loop(0, 1, work, 0)
    slots(31, 32)
    lax.fori_loop(1, 2, work, 0)
    slots(32, 33)
    lax.fori_loop(2, 3, work, 0)
    slots(33, 34)
    lax.fori_loop(3, 4, work, 0)
    slots(34, 35)
    lax.fori_loop(4, 5, work, 0)
    slots(35, 36)
    lax.fori_loop(5, 8, work, 0)

    @pl.when(xlo == 0)
    def _():
        for h in range(2):
            out[:, h, :] = p_out[:, h * NB : (h + 1) * NB]

    finish()


def factor_and_update(col0, tile):
    dma = pltpu.SemaphoreType.DMA
    vmem = pl.BlockSpec(memory_space=pltpu.VMEM)
    return pl.pallas_call(
        gather_kernel,
        out_shape=jax.ShapeDtypeStruct((BS, 32, NB), jnp.float32),
        in_specs=[vmem, pl.BlockSpec(memory_space=pl.ANY)],
        out_specs=vmem,
        scratch_shapes=[
            pltpu.VMEM((16 * BS, LEAD), jnp.float32),
            pltpu.VMEM((BS, LEAD), jnp.float32),
            pltpu.VMEM((BS, BS), jnp.float32),
            pltpu.VMEM((2, BS, BS), jnp.float32),
            pltpu.VMEM((3, 8, 2, PIECE, BS), jnp.float32),
            pltpu.VMEM((LEAD, 2 * LEAD), jnp.float32),
            pltpu.VMEM((NB, 2 * NB), jnp.float32),
            pltpu.VMEM((BS, 32, NB), jnp.float32),
            pltpu.VMEM((32, BS, NB), jnp.float32),
            dma((1,)), dma((2,)), dma((1,)), dma((1,)),
            dma((1,)), dma((3,)), dma((2,)), dma((2,)), dma((2,)), dma((2,)),
            dma((2, 4, 6)), dma((2, 4, 6)), dma((2, 4, 2, 3)), dma((2, 4, 2, 3)), dma((2, 3)), dma((2, 3)), dma((2, 4, 4)), dma((2, 4, 4)),
            dma((2,)),
        ],
        compiler_params=pltpu.CompilerParams(
            has_side_effects=True, collective_id=0, vmem_limit_bytes=46 << 20
        ),
        cost_estimate=pl.CostEstimate(
            flops=2 * BS * LEAD * 16 * BS, bytes_accessed=16 << 20, transcendentals=LEAD
        ),
    )(col0, tile)


def on_device(matrix):
    tile = matrix.reshape(BS, 64, NB)
    col0 = tile[:, 0:2, :].reshape(BS, BS)
    return factor_and_update(col0, tile).reshape(1, 1, BS, 16, 1, BS)


def solution(mesh):
    in_specs = (P(None, "row", None, None, "col", None),)
    out_specs = P(None, "row", None, "layer", "col", None)
    return jax.shard_map(
        on_device, mesh=mesh, in_specs=in_specs, out_specs=out_specs, check_vma=False
    )
```

```python
import jax
import jax.numpy as jnp
from jax import lax
from jax.experimental import pallas as pl
from jax.experimental.pallas import tpu as pltpu
from jax.sharding import PartitionSpec as P

HIGH = lax.Precision.HIGHEST
BS = 256
LEAD = 2 * BS
NB = 128
ZROWS = 40
YROWS = 48
YBASE = 2 * ZROWS
EVENTS = 24
PIECE = 16
YWAIT = ((1, 2), (0, 2))
LAG = 3
SLOTS = EVENTS + 4 * LAG
FIRST = 4
MESH = pl.DeviceIdType.MESH


def dotf(a, b, ca, cb):
    return lax.dot_general(
        a, b, (((ca,), (cb,)), ((), ())), precision=HIGH, preferred_element_type=jnp.float32
    )


def parts(v):
    high = v.astype(jnp.bfloat16).astype(jnp.float32)
    rest = v - high
    mid = rest.astype(jnp.bfloat16).astype(jnp.float32)
    low = (rest - mid).astype(jnp.bfloat16).astype(jnp.float32)
    return high, mid, low


def rank8(left, both):
    a, b, c = parts(left)
    d, e, f = parts(both)
    return lax.dot_general(
        jnp.concatenate([a, a, b, a, c, b], axis=0),
        jnp.concatenate([d, e, d, f, d, e], axis=0),
        (((0,), (0,)), ((), ())),
        preferred_element_type=jnp.float32,
    )


def down(v, i):
    return jnp.broadcast_to(v[i : i + 1, :], (8, NB))


def across(v, j):
    return jnp.broadcast_to(v[:, j : j + 1], (8, NB))


def diag_factor(dx, between):
    sub = lax.broadcasted_iota(jnp.int32, (8, NB), 0)
    left = dx[0:8, 0:NB]
    right = dx[0:8, NB : 2 * NB]
    for p in range(NB // 8):
        lo = 8 * p
        ahead = p < NB // 8 - 1
        cols = [across(left, lo + i) for i in range(8)]
        if ahead:
            left2 = dx[lo + 8 : lo + 16, 0:NB]
            right2 = dx[lo + 8 : lo + 16, NB : 2 * NB]
            cols2 = [across(left2, lo + i) for i in range(8)]
        scale = None
        for i in range(8):
            root = lax.rsqrt(down(cols[i], i))
            inv = root * root
            scale = root if scale is None else jnp.where(sub == i, root, scale)
            below = jnp.where(sub > i, cols[i], 0.0)
            for k in range(i + 1, 8):
                row = down(cols[k], i) * inv
                cols[k] = cols[k] - below * row
                if ahead:
                    cols2[k] = cols2[k] - cols2[i] * row
            row_l = down(left, i) * inv
            row_r = down(right, i) * inv
            left = left - below * row_l
            right = right - below * row_r
            if ahead:
                left2 = left2 - cols2[i] * row_l
                right2 = right2 - cols2[i] * row_r
        left = left * scale
        both = jnp.concatenate([left, right * scale], axis=1)
        dx[lo : lo + 8, :] = both
        if lo + 16 < NB:
            upd = rank8(left, both)
            dx[lo + 16 :, :] = dx[lo + 16 :, :] - upd[lo + 16 :, :]
        if ahead:
            left, right = left2, right2
        between(p)


def gather_kernel(
    col0, tile, out, g, q_out, p_out, w, abuf, m, dx, raw, own,
    inj_send, inj_recv, w_send, w_recv,
    sc_send, sc_recv, ag_send, ag_recv, sib_send, sib_recv,
    z_send, z_recv, yz_send, yz_recv, yy_send, yy_recv, x_send, x_recv, loc,
):
    row = lax.axis_index("row")
    core = lax.axis_index("col")
    xlo = lax.axis_index("layer")
    z = row // 8
    y = (row // 2) % 4
    xhi = row % 2
    x = xhi * 2 + xlo
    n = z * 4 + y

    def dev(dz, dy, dx_, dc):
        high = jnp.where(dx_ >= 2, 1, 0)
        return {"row": dz * 8 + dy * 2 + high, "col": dc, "layer": dx_ - 2 * high}

    def remote(src, dst, ss, rs, to):
        return pltpu.make_async_remote_copy(
            src_ref=src, dst_ref=dst, send_sem=ss, recv_sem=rs, device_id=to, device_id_type=MESH
        )

    sibling = dev(z, y, x, 1 - core)

    unit = xhi + core
    is_src = (row < 2) & ((xhi == 0) | (core == 1))
    own_src = (row == 0) & (core == 0)
    match = (n % 2 == 0) & ((n // 2) % 2 == core)
    zhalf = z // 4
    same = xlo == zhalf
    ring = (
        dev((z + 1) % 8, y, x, core),
        dev((z + 7) % 8, y, x, core),
        dev(z, (y + 1) % 4, x, core),
        dev(z, (y + 3) % 4, x, core),
    )

    barrier = pltpu.get_barrier_semaphore()

    def greet(to):
        pl.semaphore_signal(barrier, inc=1, device_id=to, device_id_type=MESH)

    twin = dev(z, y, (x + 2) % 4, core)
    native = core == xhi
    for to in ring + (sibling, twin):
        greet(to)

    @pl.when(match)
    def _():
        low = jnp.where(xhi == 0, x, 3 - x)

        @pl.when(jnp.logical_not(own_src))
        def _():
            greet(dev(0, 0, low, 0))

        greet(dev(0, 0, low, 1))
        greet(dev(0, 0, 3 - low, 1))

    @pl.when(same & (core != xhi))
    def _():
        greet(dev(z, y, 3 - x, 0))
        greet(dev(z, y, 3 - x, 1))

    def greet_holder(i, _):
        holder = 4 * i + 2 * core

        @pl.when(holder != n)
        def _():
            greet(dev(holder // 4, holder % 4, x, core))

        return 0

    lax.fori_loop(0, 8, greet_holder, 0)
    pl.semaphore_wait(
        barrier,
        6
        + jnp.where(match, 31, 0)
        + jnp.where(is_src, 32, 0)
        - jnp.where(own_src, 1, 0)
        + jnp.where(same, 0, 1),
    )

    @pl.when(is_src)
    def _():
        for i in range(16):
            src = col0.at[PIECE * i : PIECE * (i + 1), :]
            dst = abuf.at[unit, i // 2, i % 2]
            hz, hy = i // 2, 2 * (i % 2)
            here = remote(src, dst, sc_send.at[0], sc_recv.at[unit], dev(hz, hy, x, i % 2))
            if i == 0:
                @pl.when(own_src)
                def _():
                    pltpu.make_async_copy(src, dst, sc_recv.at[unit]).start()

                @pl.when(jnp.logical_not(own_src))
                def _():
                    here.start()
            else:
                here.start()
            remote(src, dst, sc_send.at[0], sc_recv.at[unit], dev(hz, hy, 3 - x, i % 2)).start()

    inj_x = jnp.where(same, x, 3 - x)
    inj_self = same & (xhi == core)
    zown = z % 4
    own_slot = zown * 4 + y
    inj_dst = g.at[pl.ds(pl.multiple_of(own_slot * BS, BS), BS), pl.ds(pl.multiple_of(core * BS, BS), BS)]
    inj = remote(col0, inj_dst, inj_send.at[0], inj_recv.at[core], dev(z, y, inj_x, xhi))
    inj_local = pltpu.make_async_copy(col0, inj_dst, inj_recv.at[core])

    @pl.when(inj_self)
    def _():
        inj_local.start()

    @pl.when(jnp.logical_not(inj_self))
    def _():
        inj.start()

    w_copy = remote(col0, w.at[core], w_send.at[0], w_recv.at[0], sibling)
    w_copy.start()
    w_local = pltpu.make_async_copy(col0, w.at[core], loc.at[0])
    w_local.start()
    tile_copy = pltpu.make_async_copy(tile.at[:, pl.ds(pl.multiple_of(xlo * 32, 32), 32), :], raw, loc.at[1])
    tile_copy.start()

    def spread(which, first, count):
        @pl.when(match)
        def _():
            for u in range(first, first + count):
                pltpu.make_async_copy(
                    abuf.at[u, n // 4, core], abuf.at[u, n // 4, core], sc_recv.at[u]
                ).wait()
            piece = abuf.at[pl.ds(first, count), n // 4, core]

            def one(i, _):
                other = (n + i) % 32
                remote(piece, piece, ag_send.at[which], ag_recv.at[which], dev(other // 4, other % 4, x, core)).start()
                return 0

            lax.fori_loop(1, 32, one, 0)


    def bytes_wait(sem, pieces):
        ref = m.at[0 : 8 * pieces, 0:LEAD]
        pltpu.make_async_copy(ref, ref, sem).wait()

    def sib_copy(which, first, count):
        half = abuf.at[pl.ds(first, count), :, core]
        return remote(half, half, sib_send.at[which], sib_recv.at[which], sibling)

    def lead_half(which, first, count):
        @pl.when(match)
        def _():
            bytes_wait(ag_recv.at[which], 7 * count)

        @pl.when(jnp.logical_not(match))
        def _():
            bytes_wait(ag_recv.at[which], 8 * count)

        sib_copy(which, first, count).start()

    zp = (z + 8 - 4 * xlo) % 8
    near = zp < 4
    far = jnp.logical_not(near)
    zd = (zp, (11 - zp) % 8)
    base = tuple(jnp.where(v < 4, v, 3) for v in zd)
    nsend = tuple(jnp.where((v <= 2) | (v == 7), 3, 4) for v in zd)
    zto = (dev((z + 1) % 8, y, x, core), dev((z + 7) % 8, y, x, core))
    yup = dev(z, (y + 1) % 4, x, core)
    ydown = dev(z, (y + 3) % 4, x, core)
    yto = (yup, ydown)
    yfrom = ((y + 3) % 4, (y + 1) % 4)

    def event_at(v, t):
        turn = 6 * (v + 1)
        late = t - ((5 + v) * LAG - turn)
        wrap = jnp.where(late >= turn, late, -1)
        return jnp.where(v < 4, jnp.where((t < turn) | (v == 3), t, wrap), t - LAG * (v - 3))

    def wrap4(v):
        return jnp.where(v >= 4, v - 4, v)

    def source_z(d, q):
        s = wrap4(base[d] + 4 - q)
        return s if d == 0 else 3 - s

    def part(zs, ys, first, rows):
        start = (zs * 4 + ys) * BS + first
        return g.at[pl.ds(pl.multiple_of(start, 8), rows), :]

    def zpart(d, q, j, ys):
        return part(source_z(d, q), ys, NB * d + ZROWS * j, ZROWS)

    def ypart(d, zs, ys):
        return part(zs, ys, NB * d + YBASE, YROWS)

    def zcopy(d, q, j, ref):
        return remote(ref, ref, z_send.at[d, q, j], z_recv.at[d, q, j], zto[d])

    def yz_copy(d, q, j, s, ref, to):
        return remote(ref, ref, yz_send.at[d, q, j, s], yz_recv.at[d, q, j, s], to)

    def x_copy(d, q, j, ref):
        return remote(ref, ref, x_send.at[d, q, j], x_recv.at[d, q, j], twin)

    def yy_copy(d, s, ref, to):
        return remote(ref, ref, yy_send.at[d, s], yy_recv.at[d, s], to)

    def unpack(first, last):
        if first == 0:
            tile_copy.wait()
        for v in range(first, last):
            own[v] = raw[:, v, :]

    def near_start():
        @pl.when(near)
        def _():
            for h in range(2):
                pltpu.make_async_copy(col0, col0, inj_recv.at[h]).wait()
            for d in range(2):
                ref = ypart(d, zown, y)
                yy_copy(d, 0, ref, yup).start()
                yy_copy(d, 1, ref, ydown).start()

    def near_forward():
        @pl.when(near)
        def _():
            for d in range(2):
                ref = ypart(d, zown, yfrom[d])
                yy_copy(d, d, ref, yto[d]).wait_recv()
                yy_copy(d, 2, ref, yto[d]).start()

    def pass_on(d, q, j, ref):
        @pl.when(far | (q > 0))
        def _():
            arrived = jnp.where(near, q - 1, q)
            pltpu.make_async_copy(ref, ref, z_recv.at[d, jnp.maximum(arrived, 0), j]).wait()

        @pl.when(q < nsend[d])
        def _():
            zcopy(d, q, j, ref).start()

    def event(d, e):
        q = jnp.where(e >= 18, 3, jnp.where(e >= 12, 2, jnp.where(e >= 6, 1, 0)))
        j = e - 6 * q

        @pl.when(j < 2)
        def _():
            ref = zpart(d, q, j, y)
            pass_on(d, q, j, ref)
            yz_copy(d, q, j, 0, ref, yup).start()
            yz_copy(d, q, j, 1, ref, ydown).start()

        @pl.when((j >= 2) & native)
        def _():
            i = j - 2
            gray = jnp.where(i == 2, 3, jnp.where(i == 3, 2, i))
            ref = ypart(d, source_z(d, q), wrap4(y + gray))

            for num, s in ((1, 1), (2, 0), (3, 2)):
                if s != d:
                    @pl.when(near & (q == 0) & (i == num))
                    def _():
                        pltpu.make_async_copy(ref, ref, yy_recv.at[d, s]).wait()

            pass_on(d, q, j, ref)

            @pl.when(far | (q > 0))
            def _():
                x_copy(d, q, i, ref).start()

        @pl.when((j == 3) | (j == 4))
        def _():
            ref = zpart(d, q, j - 3, yfrom[d])
            yz_copy(d, q, j - 3, d, ref, yto[d]).wait_recv()
            yz_copy(d, q, j - 3, 2, ref, yto[d]).start()

    def slot(t):
        t = jnp.int32(t)
        for d in range(2):
            e = event_at(zd[d], t)

            @pl.when((e >= 0) & (e < EVENTS))
            def _():
                event(d, e)

        @pl.when(jnp.int32(t) == 2)
        def _():
            near_forward()

    def finish():
        inj_wait = jnp.logical_not(inj_self)

        @pl.when(inj_wait)
        def _():
            inj.wait_send()

        w_copy.wait_send()

        @pl.when(is_src)
        def _():
            @pl.when(own_src)
            def _():
                bytes_wait(sc_send.at[0], 31)

            @pl.when(jnp.logical_not(own_src))
            def _():
                bytes_wait(sc_send.at[0], 32)

        @pl.when(match)
        def _():
            bytes_wait(ag_send.at[0], 31)
            bytes_wait(ag_send.at[1], 62)

        for which, first, count in ((0, 0, 1), (1, 1, 2)):
            sib_copy(which, first, count).wait_send()

        @pl.when(near)
        def _():
            for d in range(2):
                for s in range(3):
                    yy_copy(d, s, ypart(d, zown, y), yup).wait_send()

        def each(q, _):
            for d in range(2):
                for j in range(2):
                    for s in range(3):
                        copy = yz_copy(d, q, j, s, zpart(d, q, j, y), yup)
                        copy.wait_send()

                @pl.when(q < nsend[d])
                def _():
                    for j in range(2):
                        zcopy(d, q, j, zpart(d, q, j, y)).wait_send()

                @pl.when(native)
                def _():
                    ref = ypart(d, source_z(d, q), y)
                    for j in range(4):
                        @pl.when(q < nsend[d])
                        def _():
                            zcopy(d, q, 2 + j, ref).wait_send()

                        @pl.when(far | (q > 0))
                        def _():
                            x_copy(d, q, j, ref).wait_send()
            return 0

        lax.fori_loop(0, 4, each, 0)

    spread(0, 0, 1)
    near_start()
    slot(0)
    slot(1)
    lead_half(0, 0, 1)
    slot(2)
    spread(1, 1, 2)
    unpack(0, 32)
    slot(3)

    eye = (
        lax.broadcasted_iota(jnp.int32, (LEAD, LEAD), 0)
        == lax.broadcasted_iota(jnp.int32, (LEAD, LEAD), 1)
    ).astype(jnp.float32)
    m[:, LEAD:] = eye
    sib_copy(0, 0, 1).wait_recv()
    m[0:BS, 0:BS] = abuf[0].reshape(BS, BS)
    m[BS:LEAD, 0:BS] = jnp.zeros((BS, BS), jnp.float32)

    def step(k, _):
        off = pl.multiple_of(k * NB, NB)
        dx[:, 0:NB] = m[pl.ds(off, NB), pl.ds(off, NB)]
        dx[:, NB : 2 * NB] = eye[0:NB, 0:NB]

        def between(p):
            if p % 3 == 0 and p < 18:
                slot(FIRST + 6 * k + p // 3)
            if p == 8:
                @pl.when(k == 0)
                def _():
                    lead_half(1, 1, 2)

        diag_factor(dx, between)

        @pl.when(k == 0)
        def _():
            sib_copy(1, 1, 2).wait_recv()
            m[0:BS, BS:LEAD] = abuf[1].reshape(BS, BS)
            m[BS:LEAD, BS:LEAD] = abuf[2].reshape(BS, BS)

        span = pl.ds(off, LEAD + NB)
        mk = dotf(dx[:, NB : 2 * NB], m[pl.ds(off, NB), span], 1, 0)
        m[pl.ds(off, NB), span] = mk

        def trail(i, _):
            oi = pl.multiple_of(i * NB, NB)
            u = m[pl.ds(off, NB), pl.ds(oi, NB)]
            m[pl.ds(oi, NB), span] = m[pl.ds(oi, NB), span] - dotf(u, mk, 0, 0)
            return 0

        lax.fori_loop(k + 1, LEAD // NB, trail, 0)
        return 0

    lax.fori_loop(0, LEAD // NB, step, 0)

    slot(28)
    w_copy.wait_recv()
    w_local.wait()
    p0 = dotf(w[0], m[0:BS, LEAD : LEAD + BS], 1, 1)
    p1 = dotf(w[0], m[BS:LEAD, LEAD : LEAD + BS], 1, 1) + dotf(w[1], m[BS:LEAD, LEAD + BS :], 1, 1)
    q_out[:, 0:BS] = dotf(p0, m[0:BS, LEAD : LEAD + BS], 1, 0) + dotf(p1, m[BS:LEAD, LEAD : LEAD + BS], 1, 0)
    q_out[:, BS:LEAD] = dotf(p1, m[BS:LEAD, LEAD + BS :], 1, 0)
    slot(29)
    p_out[...] = jnp.where(core == 0, p0, p1)
    ri = lax.broadcasted_iota(jnp.int32, (BS, BS), 0)
    ci = lax.broadcasted_iota(jnp.int32, (BS, BS), 1)

    @pl.when((row == 0) & (core == 0))
    def _():
        p_out[...] = jnp.where(ri >= ci, m[0:BS, 0:BS].T, 0.0)

    @pl.when((row == 0) & (core == 1))
    def _():
        p_out[...] = jnp.zeros((BS, BS), jnp.float32)

    @pl.when((row == 1) & (core == 0))
    def _():
        p_out[...] = m[0:BS, BS:LEAD].T

    @pl.when((row == 1) & (core == 1))
    def _():
        p_out[...] = jnp.where(ri >= ci, m[BS:LEAD, BS:LEAD].T, 0.0)

    flat = out.reshape(BS * 32, NB)

    def work(i, _):
        q = i // 2

        @pl.when(i % 2 == 0)
        def _():
            for d in range(2):
                for j in range(2):
                    for s in range(3):
                        if s != d:
                            yz_copy(d, q, j, s, zpart(d, q, j, y), yup).wait_recv()

            @pl.when(jnp.logical_not(native))
            def _():
                for d in range(2):
                    for j in range(4):
                        ref = ypart(d, source_z(d, q), y)

                        @pl.when(far | (q > 0))
                        def _():
                            x_copy(d, q, j, ref).wait_recv()

                    for s in YWAIT[d]:
                        @pl.when(near & (q == 0))
                        def _():
                            yy_copy(d, s, ypart(d, zown, y), yup).wait_recv()

        for d in range(2):
            ids = [(source_z(d, q) * 4 + 2 * (i % 2) + h) * 2 + d for h in range(2)]
            rows = [g[pl.ds(pl.multiple_of(v * NB, NB), NB), :] for v in ids]
            upd = dotf(q_out[...], jnp.concatenate(rows, axis=0), 1, 1)
            for h in range(2):
                where = pl.ds(ids[h], BS, stride=32)
                flat[where, :] = own[ids[h]] - upd[:, h * NB : (h + 1) * NB]
        return 0

    def slots(first, last):
        lax.fori_loop(first, last, lambda t, _: (slot(t), 0)[1], 0)

    slots(30, 31)
    lax.fori_loop(0, 1, work, 0)
    slots(31, 32)
    lax.fori_loop(1, 2, work, 0)
    slots(32, 33)
    lax.fori_loop(2, 3, work, 0)
    slots(33, 34)
    lax.fori_loop(3, 4, work, 0)
    slots(34, 35)
    lax.fori_loop(4, 5, work, 0)
    slots(35, 36)
    lax.fori_loop(5, 8, work, 0)

    @pl.when(xlo == 0)
    def _():
        for h in range(2):
            out[:, h, :] = p_out[:, h * NB : (h + 1) * NB]

    finish()


def factor_and_update(col0, tile):
    dma = pltpu.SemaphoreType.DMA
    vmem = pl.BlockSpec(memory_space=pltpu.VMEM)
    return pl.pallas_call(
        gather_kernel,
        out_shape=jax.ShapeDtypeStruct((BS, 32, NB), jnp.float32),
        in_specs=[vmem, pl.BlockSpec(memory_space=pl.ANY)],
        out_specs=vmem,
        scratch_shapes=[
            pltpu.VMEM((16 * BS, LEAD), jnp.float32),
            pltpu.VMEM((BS, LEAD), jnp.float32),
            pltpu.VMEM((BS, BS), jnp.float32),
            pltpu.VMEM((2, BS, BS), jnp.float32),
            pltpu.VMEM((3, 8, 2, PIECE, BS), jnp.float32),
            pltpu.VMEM((LEAD, 2 * LEAD), jnp.float32),
            pltpu.VMEM((NB, 2 * NB), jnp.float32),
            pltpu.VMEM((BS, 32, NB), jnp.float32),
            pltpu.VMEM((32, BS, NB), jnp.float32),
            dma((1,)), dma((2,)), dma((1,)), dma((1,)),
            dma((1,)), dma((3,)), dma((2,)), dma((2,)), dma((2,)), dma((2,)),
            dma((2, 4, 6)), dma((2, 4, 6)), dma((2, 4, 2, 3)), dma((2, 4, 2, 3)), dma((2, 3)), dma((2, 3)), dma((2, 4, 4)), dma((2, 4, 4)),
            dma((2,)),
        ],
        compiler_params=pltpu.CompilerParams(
            has_side_effects=True, collective_id=0, vmem_limit_bytes=46 << 20
        ),
        cost_estimate=pl.CostEstimate(
            flops=2 * BS * LEAD * 16 * BS, bytes_accessed=16 << 20, transcendentals=LEAD
        ),
    )(col0, tile)


def on_device(matrix):
    tile = matrix.reshape(BS, 64, NB)
    col0 = tile[:, 0:2, :].reshape(BS, BS)
    return factor_and_update(col0, tile).reshape(1, 1, BS, 16, 1, BS)


def solution(mesh):
    in_specs = (P(None, "row", None, None, "col", None),)
    out_specs = P(None, "row", None, "layer", "col", None)
    return jax.shard_map(
        on_device, mesh=mesh, in_specs=in_specs, out_specs=out_specs, check_vma=False
    )
```

```python
import jax
import jax.numpy as jnp
from jax import lax
from jax.experimental import pallas as pl
from jax.experimental.pallas import tpu as pltpu
from jax.sharding import PartitionSpec as P

HIGH = lax.Precision.HIGHEST
BS = 256
LEAD = 2 * BS
NB = 128
ZROWS = 40
YROWS = 48
YBASE = 2 * ZROWS
EVENTS = 24
PIECE = 16
YWAIT = ((1, 2), (0, 2))
LAG = 3
SLOTS = EVENTS + 4 * LAG
FIRST = 4
MESH = pl.DeviceIdType.MESH


def dotf(a, b, ca, cb):
    return lax.dot_general(
        a, b, (((ca,), (cb,)), ((), ())), precision=HIGH, preferred_element_type=jnp.float32
    )


def parts(v):
    high = v.astype(jnp.bfloat16).astype(jnp.float32)
    rest = v - high
    mid = rest.astype(jnp.bfloat16).astype(jnp.float32)
    low = (rest - mid).astype(jnp.bfloat16).astype(jnp.float32)
    return high, mid, low


def rank8(left, both):
    a, b, c = parts(left)
    d, e, f = parts(both)
    return lax.dot_general(
        jnp.concatenate([a, a, b, a, c, b], axis=0),
        jnp.concatenate([d, e, d, f, d, e], axis=0),
        (((0,), (0,)), ((), ())),
        preferred_element_type=jnp.float32,
    )


def down(v, i):
    return jnp.broadcast_to(v[i : i + 1, :], (8, NB))


def across(v, j):
    return jnp.broadcast_to(v[:, j : j + 1], (8, NB))


def diag_factor(dx, between):
    sub = lax.broadcasted_iota(jnp.int32, (8, NB), 0)
    left = dx[0:8, 0:NB]
    right = dx[0:8, NB : 2 * NB]
    for p in range(NB // 8):
        lo = 8 * p
        ahead = p < NB // 8 - 1
        cols = [across(left, lo + i) for i in range(8)]
        if ahead:
            left2 = dx[lo + 8 : lo + 16, 0:NB]
            right2 = dx[lo + 8 : lo + 16, NB : 2 * NB]
            cols2 = [across(left2, lo + i) for i in range(8)]
        scale = None
        for i in range(8):
            root = lax.rsqrt(down(cols[i], i))
            inv = root * root
            scale = root if scale is None else jnp.where(sub == i, root, scale)
            below = jnp.where(sub > i, cols[i], 0.0)
            for k in range(i + 1, 8):
                row = down(cols[k], i) * inv
                cols[k] = cols[k] - below * row
                if ahead:
                    cols2[k] = cols2[k] - cols2[i] * row
            row_l = down(left, i) * inv
            row_r = down(right, i) * inv
            left = left - below * row_l
            right = right - below * row_r
            if ahead:
                left2 = left2 - cols2[i] * row_l
                right2 = right2 - cols2[i] * row_r
        left = left * scale
        both = jnp.concatenate([left, right * scale], axis=1)
        dx[lo : lo + 8, :] = both
        if lo + 16 < NB:
            upd = rank8(left, both)
            dx[lo + 16 :, :] = dx[lo + 16 :, :] - upd[lo + 16 :, :]
        if ahead:
            left, right = left2, right2
        between(p)


def gather_kernel(
    col0, tile, out, g, q_out, p_out, w, abuf, m, dx, raw, own,
    inj_send, inj_recv, w_send, w_recv,
    sc_send, sc_recv, ag_send, ag_recv, sib_send, sib_recv,
    z_send, z_recv, yz_send, yz_recv, yy_send, yy_recv, x_send, x_recv, loc,
):
    row = lax.axis_index("row")
    core = lax.axis_index("col")
    xlo = lax.axis_index("layer")
    z = row // 8
    y = (row // 2) % 4
    xhi = row % 2
    x = xhi * 2 + xlo
    n = z * 4 + y

    def dev(dz, dy, dx_, dc):
        high = jnp.where(dx_ >= 2, 1, 0)
        return {"row": dz * 8 + dy * 2 + high, "col": dc, "layer": dx_ - 2 * high}

    def remote(src, dst, ss, rs, to):
        return pltpu.make_async_remote_copy(
            src_ref=src, dst_ref=dst, send_sem=ss, recv_sem=rs, device_id=to, device_id_type=MESH
        )

    sibling = dev(z, y, x, 1 - core)

    unit = xhi + core
    is_src = (row < 2) & ((xhi == 0) | (core == 1))
    own_src = (row == 0) & (core == 0)
    match = (n % 2 == 0) & ((n // 2) % 2 == core)
    zhalf = z // 4
    same = xlo == zhalf
    ring = (
        dev((z + 1) % 8, y, x, core),
        dev((z + 7) % 8, y, x, core),
        dev(z, (y + 1) % 4, x, core),
        dev(z, (y + 3) % 4, x, core),
    )

    barrier = pltpu.get_barrier_semaphore()

    def greet(to):
        pl.semaphore_signal(barrier, inc=1, device_id=to, device_id_type=MESH)

    twin = dev(z, y, (x + 2) % 4, core)
    native = core == xhi
    for to in ring + (sibling, twin):
        greet(to)

    @pl.when(match)
    def _():
        low = jnp.where(xhi == 0, x, 3 - x)

        @pl.when(jnp.logical_not(own_src))
        def _():
            greet(dev(0, 0, low, 0))

        greet(dev(0, 0, low, 1))
        greet(dev(0, 0, 3 - low, 1))

    @pl.when(same & (core != xhi))
    def _():
        greet(dev(z, y, 3 - x, 0))
        greet(dev(z, y, 3 - x, 1))

    def greet_holder(i, _):
        holder = 4 * i + 2 * core

        @pl.when(holder != n)
        def _():
            greet(dev(holder // 4, holder % 4, x, core))

        return 0

    lax.fori_loop(0, 8, greet_holder, 0)
    pl.semaphore_wait(
        barrier,
        6
        + jnp.where(match, 31, 0)
        + jnp.where(is_src, 32, 0)
        - jnp.where(own_src, 1, 0)
        + jnp.where(same, 0, 1),
    )

    @pl.when(is_src)
    def _():
        for i in range(16):
            src = col0.at[PIECE * i : PIECE * (i + 1), :]
            dst = abuf.at[unit, i // 2, i % 2]
            hz, hy = i // 2, 2 * (i % 2)
            here = remote(src, dst, sc_send.at[0], sc_recv.at[unit], dev(hz, hy, x, i % 2))
            if i == 0:
                @pl.when(own_src)
                def _():
                    pltpu.make_async_copy(src, dst, sc_recv.at[unit]).start()

                @pl.when(jnp.logical_not(own_src))
                def _():
                    here.start()
            else:
                here.start()
            remote(src, dst, sc_send.at[0], sc_recv.at[unit], dev(hz, hy, 3 - x, i % 2)).start()

    inj_x = jnp.where(same, x, 3 - x)
    inj_self = same & (xhi == core)
    zown = z % 4
    own_slot = zown * 4 + y
    inj_dst = g.at[pl.ds(pl.multiple_of(own_slot * BS, BS), BS), pl.ds(pl.multiple_of(core * BS, BS), BS)]
    inj = remote(col0, inj_dst, inj_send.at[0], inj_recv.at[core], dev(z, y, inj_x, xhi))
    inj_local = pltpu.make_async_copy(col0, inj_dst, inj_recv.at[core])

    @pl.when(inj_self)
    def _():
        inj_local.start()

    @pl.when(jnp.logical_not(inj_self))
    def _():
        inj.start()

    w_copy = remote(col0, w.at[core], w_send.at[0], w_recv.at[0], sibling)
    w_copy.start()
    w_local = pltpu.make_async_copy(col0, w.at[core], loc.at[0])
    w_local.start()
    tile_copy = pltpu.make_async_copy(tile.at[:, pl.ds(pl.multiple_of(xlo * 32, 32), 32), :], raw, loc.at[1])
    tile_copy.start()

    def spread(which, first, count):
        @pl.when(match)
        def _():
            for u in range(first, first + count):
                pltpu.make_async_copy(
                    abuf.at[u, n // 4, core], abuf.at[u, n // 4, core], sc_recv.at[u]
                ).wait()
            piece = abuf.at[pl.ds(first, count), n // 4, core]

            def one(i, _):
                other = (n + i) % 32
                remote(piece, piece, ag_send.at[which], ag_recv.at[which], dev(other // 4, other % 4, x, core)).start()
                return 0

            lax.fori_loop(1, 32, one, 0)


    def bytes_wait(sem, pieces):
        ref = m.at[0 : 8 * pieces, 0:LEAD]
        pltpu.make_async_copy(ref, ref, sem).wait()

    def sib_copy(which, first, count):
        half = abuf.at[pl.ds(first, count), :, core]
        return remote(half, half, sib_send.at[which], sib_recv.at[which], sibling)

    def lead_half(which, first, count):
        @pl.when(match)
        def _():
            bytes_wait(ag_recv.at[which], 7 * count)

        @pl.when(jnp.logical_not(match))
        def _():
            bytes_wait(ag_recv.at[which], 8 * count)

        sib_copy(which, first, count).start()

    zp = (z + 8 - 4 * xlo) % 8
    near = zp < 4
    far = jnp.logical_not(near)
    zd = (zp, (11 - zp) % 8)
    base = tuple(jnp.where(v < 4, v, 3) for v in zd)
    nsend = tuple(jnp.where((v <= 2) | (v == 7), 3, 4) for v in zd)
    zto = (dev((z + 1) % 8, y, x, core), dev((z + 7) % 8, y, x, core))
    yup = dev(z, (y + 1) % 4, x, core)
    ydown = dev(z, (y + 3) % 4, x, core)
    yto = (yup, ydown)
    yfrom = ((y + 3) % 4, (y + 1) % 4)

    def event_at(v, t):
        turn = 6 * (v + 1)
        late = t - ((5 + v) * LAG - turn)
        wrap = jnp.where(late >= turn, late, -1)
        return jnp.where(v < 4, jnp.where((t < turn) | (v == 3), t, wrap), t - LAG * (v - 3))

    def wrap4(v):
        return jnp.where(v >= 4, v - 4, v)

    def source_z(d, q):
        s = wrap4(base[d] + 4 - q)
        return s if d == 0 else 3 - s

    def part(zs, ys, first, rows):
        start = (zs * 4 + ys) * BS + first
        return g.at[pl.ds(pl.multiple_of(start, 8), rows), :]

    def zpart(d, q, j, ys):
        return part(source_z(d, q), ys, NB * d + ZROWS * j, ZROWS)

    def ypart(d, zs, ys):
        return part(zs, ys, NB * d + YBASE, YROWS)

    def zcopy(d, q, j, ref):
        return remote(ref, ref, z_send.at[d, q, j], z_recv.at[d, q, j], zto[d])

    def yz_copy(d, q, j, s, ref, to):
        return remote(ref, ref, yz_send.at[d, q, j, s], yz_recv.at[d, q, j, s], to)

    def x_copy(d, q, j, ref):
        return remote(ref, ref, x_send.at[d, q, j], x_recv.at[d, q, j], twin)

    def yy_copy(d, s, ref, to):
        return remote(ref, ref, yy_send.at[d, s], yy_recv.at[d, s], to)

    def unpack(first, last):
        if first == 0:
            tile_copy.wait()
        for v in range(first, last):
            own[v] = raw[:, v, :]

    def near_start():
        @pl.when(near)
        def _():
            for h in range(2):
                pltpu.make_async_copy(col0, col0, inj_recv.at[h]).wait()
            for d in range(2):
                ref = ypart(d, zown, y)
                yy_copy(d, 0, ref, yup).start()
                yy_copy(d, 1, ref, ydown).start()

    def near_forward():
        @pl.when(near)
        def _():
            for d in range(2):
                ref = ypart(d, zown, yfrom[d])
                yy_copy(d, d, ref, yto[d]).wait_recv()
                yy_copy(d, 2, ref, yto[d]).start()

    def pass_on(d, q, j, ref):
        @pl.when(far | (q > 0))
        def _():
            arrived = jnp.where(near, q - 1, q)
            pltpu.make_async_copy(ref, ref, z_recv.at[d, jnp.maximum(arrived, 0), j]).wait()

        @pl.when(q < nsend[d])
        def _():
            zcopy(d, q, j, ref).start()

    def event(d, e):
        q = jnp.where(e >= 18, 3, jnp.where(e >= 12, 2, jnp.where(e >= 6, 1, 0)))
        j = e - 6 * q

        @pl.when(j < 2)
        def _():
            ref = zpart(d, q, j, y)
            pass_on(d, q, j, ref)
            yz_copy(d, q, j, 0, ref, yup).start()
            yz_copy(d, q, j, 1, ref, ydown).start()

        @pl.when((j >= 2) & native)
        def _():
            i = j - 2
            gray = jnp.where(i == 2, 3, jnp.where(i == 3, 2, i))
            ref = ypart(d, source_z(d, q), wrap4(y + gray))

            for num, s in ((1, 1), (2, 0), (3, 2)):
                if s != d:
                    @pl.when(near & (q == 0) & (i == num))
                    def _():
                        pltpu.make_async_copy(ref, ref, yy_recv.at[d, s]).wait()

            pass_on(d, q, j, ref)

            @pl.when(far | (q > 0))
            def _():
                x_copy(d, q, i, ref).start()

        @pl.when((j == 3) | (j == 4))
        def _():
            ref = zpart(d, q, j - 3, yfrom[d])
            yz_copy(d, q, j - 3, d, ref, yto[d]).wait_recv()
            yz_copy(d, q, j - 3, 2, ref, yto[d]).start()

    def slot(t):
        t = jnp.int32(t)
        for d in range(2):
            e = event_at(zd[d], t)

            @pl.when((e >= 0) & (e < EVENTS))
            def _():
                event(d, e)

        @pl.when(jnp.int32(t) == 2)
        def _():
            near_forward()

    def finish():
        inj_wait = jnp.logical_not(inj_self)

        @pl.when(inj_wait)
        def _():
            inj.wait_send()

        w_copy.wait_send()

        @pl.when(is_src)
        def _():
            @pl.when(own_src)
            def _():
                bytes_wait(sc_send.at[0], 31)

            @pl.when(jnp.logical_not(own_src))
            def _():
                bytes_wait(sc_send.at[0], 32)

        @pl.when(match)
        def _():
            bytes_wait(ag_send.at[0], 31)
            bytes_wait(ag_send.at[1], 62)

        for which, first, count in ((0, 0, 1), (1, 1, 2)):
            sib_copy(which, first, count).wait_send()

        @pl.when(near)
        def _():
            for d in range(2):
                for s in range(3):
                    yy_copy(d, s, ypart(d, zown, y), yup).wait_send()

        def each(q, _):
            for d in range(2):
                for j in range(2):
                    for s in range(3):
                        copy = yz_copy(d, q, j, s, zpart(d, q, j, y), yup)
                        copy.wait_send()

                @pl.when(q < nsend[d])
                def _():
                    for j in range(2):
                        zcopy(d, q, j, zpart(d, q, j, y)).wait_send()

                @pl.when(native)
                def _():
                    ref = ypart(d, source_z(d, q), y)
                    for j in range(4):
                        @pl.when(q < nsend[d])
                        def _():
                            zcopy(d, q, 2 + j, ref).wait_send()

                        @pl.when(far | (q > 0))
                        def _():
                            x_copy(d, q, j, ref).wait_send()
            return 0

        lax.fori_loop(0, 4, each, 0)

    spread(0, 0, 1)
    near_start()
    slot(0)
    lead_half(0, 0, 1)
    slot(1)
    spread(1, 1, 2)
    slot(2)
    unpack(0, 32)
    slot(3)

    eye = (
        lax.broadcasted_iota(jnp.int32, (LEAD, LEAD), 0)
        == lax.broadcasted_iota(jnp.int32, (LEAD, LEAD), 1)
    ).astype(jnp.float32)
    m[:, LEAD:] = eye
    sib_copy(0, 0, 1).wait_recv()
    m[0:BS, 0:BS] = abuf[0].reshape(BS, BS)
    m[BS:LEAD, 0:BS] = jnp.zeros((BS, BS), jnp.float32)

    def step(k, _):
        off = pl.multiple_of(k * NB, NB)
        dx[:, 0:NB] = m[pl.ds(off, NB), pl.ds(off, NB)]
        dx[:, NB : 2 * NB] = eye[0:NB, 0:NB]

        def between(p):
            if p % 3 == 0 and p < 18:
                slot(FIRST + 6 * k + p // 3)
            if p == 8:
                @pl.when(k == 0)
                def _():
                    lead_half(1, 1, 2)

        diag_factor(dx, between)

        @pl.when(k == 0)
        def _():
            sib_copy(1, 1, 2).wait_recv()
            m[0:BS, BS:LEAD] = abuf[1].reshape(BS, BS)
            m[BS:LEAD, BS:LEAD] = abuf[2].reshape(BS, BS)

        span = pl.ds(off, LEAD + NB)
        mk = dotf(dx[:, NB : 2 * NB], m[pl.ds(off, NB), span], 1, 0)
        m[pl.ds(off, NB), span] = mk

        def trail(i, _):
            oi = pl.multiple_of(i * NB, NB)
            u = m[pl.ds(off, NB), pl.ds(oi, NB)]
            m[pl.ds(oi, NB), span] = m[pl.ds(oi, NB), span] - dotf(u, mk, 0, 0)
            return 0

        lax.fori_loop(k + 1, LEAD // NB, trail, 0)
        return 0

    lax.fori_loop(0, LEAD // NB, step, 0)

    slot(28)
    w_copy.wait_recv()
    w_local.wait()
    p0 = dotf(w[0], m[0:BS, LEAD : LEAD + BS], 1, 1)
    p1 = dotf(w[0], m[BS:LEAD, LEAD : LEAD + BS], 1, 1) + dotf(w[1], m[BS:LEAD, LEAD + BS :], 1, 1)
    q_out[:, 0:BS] = dotf(p0, m[0:BS, LEAD : LEAD + BS], 1, 0) + dotf(p1, m[BS:LEAD, LEAD : LEAD + BS], 1, 0)
    q_out[:, BS:LEAD] = dotf(p1, m[BS:LEAD, LEAD + BS :], 1, 0)
    slot(29)
    p_out[...] = jnp.where(core == 0, p0, p1)
    ri = lax.broadcasted_iota(jnp.int32, (BS, BS), 0)
    ci = lax.broadcasted_iota(jnp.int32, (BS, BS), 1)

    @pl.when((row == 0) & (core == 0))
    def _():
        p_out[...] = jnp.where(ri >= ci, m[0:BS, 0:BS].T, 0.0)

    @pl.when((row == 0) & (core == 1))
    def _():
        p_out[...] = jnp.zeros((BS, BS), jnp.float32)

    @pl.when((row == 1) & (core == 0))
    def _():
        p_out[...] = m[0:BS, BS:LEAD].T

    @pl.when((row == 1) & (core == 1))
    def _():
        p_out[...] = jnp.where(ri >= ci, m[BS:LEAD, BS:LEAD].T, 0.0)

    flat = out.reshape(BS * 32, NB)

    def work(i, _):
        q = i // 2

        @pl.when(i % 2 == 0)
        def _():
            for d in range(2):
                for j in range(2):
                    for s in range(3):
                        if s != d:
                            yz_copy(d, q, j, s, zpart(d, q, j, y), yup).wait_recv()

            @pl.when(jnp.logical_not(native))
            def _():
                for d in range(2):
                    for j in range(4):
                        ref = ypart(d, source_z(d, q), y)

                        @pl.when(far | (q > 0))
                        def _():
                            x_copy(d, q, j, ref).wait_recv()

                    for s in YWAIT[d]:
                        @pl.when(near & (q == 0))
                        def _():
                            yy_copy(d, s, ypart(d, zown, y), yup).wait_recv()

        for d in range(2):
            ids = [(source_z(d, q) * 4 + 2 * (i % 2) + h) * 2 + d for h in range(2)]
            rows = [g[pl.ds(pl.multiple_of(v * NB, NB), NB), :] for v in ids]
            upd = dotf(q_out[...], jnp.concatenate(rows, axis=0), 1, 1)
            for h in range(2):
                where = pl.ds(ids[h], BS, stride=32)
                flat[where, :] = own[ids[h]] - upd[:, h * NB : (h + 1) * NB]
        return 0

    def slots(first, last):
        lax.fori_loop(first, last, lambda t, _: (slot(t), 0)[1], 0)

    slots(30, 31)
    lax.fori_loop(0, 1, work, 0)
    slots(31, 32)
    lax.fori_loop(1, 2, work, 0)
    slots(32, 33)
    lax.fori_loop(2, 3, work, 0)
    slots(33, 34)
    lax.fori_loop(3, 4, work, 0)
    slots(34, 35)
    lax.fori_loop(4, 5, work, 0)
    slots(35, 36)
    lax.fori_loop(5, 8, work, 0)

    @pl.when(xlo == 0)
    def _():
        for h in range(2):
            out[:, h, :] = p_out[:, h * NB : (h + 1) * NB]

    finish()


def factor_and_update(col0, tile):
    dma = pltpu.SemaphoreType.DMA
    vmem = pl.BlockSpec(memory_space=pltpu.VMEM)
    return pl.pallas_call(
        gather_kernel,
        out_shape=jax.ShapeDtypeStruct((BS, 32, NB), jnp.float32),
        in_specs=[vmem, pl.BlockSpec(memory_space=pl.ANY)],
        out_specs=vmem,
        scratch_shapes=[
            pltpu.VMEM((16 * BS, LEAD), jnp.float32),
            pltpu.VMEM((BS, LEAD), jnp.float32),
            pltpu.VMEM((BS, BS), jnp.float32),
            pltpu.VMEM((2, BS, BS), jnp.float32),
            pltpu.VMEM((3, 8, 2, PIECE, BS), jnp.float32),
            pltpu.VMEM((LEAD, 2 * LEAD), jnp.float32),
            pltpu.VMEM((NB, 2 * NB), jnp.float32),
            pltpu.VMEM((BS, 32, NB), jnp.float32),
            pltpu.VMEM((32, BS, NB), jnp.float32),
            dma((1,)), dma((2,)), dma((1,)), dma((1,)),
            dma((1,)), dma((3,)), dma((2,)), dma((2,)), dma((2,)), dma((2,)),
            dma((2, 4, 6)), dma((2, 4, 6)), dma((2, 4, 2, 3)), dma((2, 4, 2, 3)), dma((2, 3)), dma((2, 3)), dma((2, 4, 4)), dma((2, 4, 4)),
            dma((2,)),
        ],
        compiler_params=pltpu.CompilerParams(
            has_side_effects=True, collective_id=0, vmem_limit_bytes=46 << 20
        ),
        cost_estimate=pl.CostEstimate(
            flops=2 * BS * LEAD * 16 * BS, bytes_accessed=16 << 20, transcendentals=LEAD
        ),
    )(col0, tile)


def on_device(matrix):
    tile = matrix.reshape(BS, 64, NB)
    col0 = tile[:, 0:2, :].reshape(BS, BS)
    return factor_and_update(col0, tile).reshape(1, 1, BS, 16, 1, BS)


def solution(mesh):
    in_specs = (P(None, "row", None, None, "col", None),)
    out_specs = P(None, "row", None, "layer", "col", None)
    return jax.shard_map(
        on_device, mesh=mesh, in_specs=in_specs, out_specs=out_specs, check_vma=False
    )
```
